32 devices in a mesh: grp: 2 (over x), ctx: 4 (over y, core), head: 4 (over z).
Axes of the slice: x: 2, y: 2, z: 4, core: 2. Of those that a mesh axis runs over, the one named last changes fastest.
Arguments:
- queries: bfloat16 [4096, 1024], P(('grp', 'ctx'), 'head'), parts along dimension 0, may hold values from -8 to 8
- keys: bfloat16 [4096, 1024], P(('grp', 'ctx'), 'head'), parts along dimension 0, may hold values from -8 to 8
- values: bfloat16 [4096, 1024], P(('grp', 'ctx'), 'head'), parts along dimension 0, may hold values from -6 to 6
- grad_out: bfloat16 [4096, 1024], P(('grp', 'ctx'), 'head'), parts along dimension 0, may hold values from -96 to 96
- block_docs: int32 [32], P('grp'), parts along dimension 0, may hold values from 0 to 7, never falling along the last dimension, each value on 1 to 6 neighbouring positions
- block_order: int32 [32], P('grp'), parts along dimension 0, may hold values from 0 to 15, as said below
Outputs:
- grad_queries: bfloat16 [4096, 1024], P(('grp', 'ctx'), 'head'), parts along dimension 0
- grad_keys: bfloat16 [4096, 1024], P(('grp', 'ctx'), 'head'), parts along dimension 0
- grad_values: bfloat16 [4096, 1024], P(('grp', 'ctx'), 'head'), parts along dimension 0
The draws below stay inside these ranges and needn't reach their ends.
There are 2 independent parts, one for each index of `grp`. The reference program is written for one: setup_inputs(seed, part) draws one part's arguments, and reference() takes and returns one part's arrays. A program takes and returns all parts, laid end to end along the dimension named above; each array names one. Nothing has to cross between parts.
Inputs may be any that keep to these rules, and one draw needn't show every extreme that they name: `block_docs`: never falling along the pack; every shot covers 1 to 6 blocks, one exactly 6. `block_order`: every block exactly once; the 4 positions p with the same p // 4 take at most 1 blocks b with the same b // 4, and some such pair takes exactly 1.
All inputs are finite; a program needn't handle non-finite values.
Results may differ from the reference program's by a relative error of at most 0.0092.
Values may be sent and summed in bfloat16 or wider, within the bound.
No kernel may reach another device: no remote copies, remote signals or barrier semaphores. Data moves between devices by JAX's collectives and lax.ppermute only.
A program may use at most 64 MiB of HBM per device.

```python
import math
import jax
import jax.numpy as jnp
import numpy as np
from jax import lax

HEADS = 8
HEAD_DIM = 128
WIDTH = 1024
BLOCK = 128
BLK_DEV = 4
DOCS = 8
NBLK = 16
TOKENS = 2048
MOST_BLK = 6
N_CTX = 4


def draw_queries(key, part):
    own_key = jax.random.fold_in(key, 3)
    base = jnp.clip(jax.random.normal(own_key, (TOKENS, WIDTH), jnp.float32), -6.0, 6.0)
    return base.astype(jnp.bfloat16)


def draw_keys(key, part):
    own_key = jax.random.fold_in(key, 5)
    base = jnp.clip(jax.random.normal(own_key, (TOKENS, WIDTH), jnp.float32), -6.0, 6.0)
    return base.astype(jnp.bfloat16)


def draw_block_order(key, part):
    own_key = jax.random.fold_in(key, 7)
    offset_key, label_key, column_key, block_key, mixing_key = jax.random.split(own_key, 5)
    offset_range = N_CTX * ((BLK_DEV + N_CTX - 1) // N_CTX)
    offsets = jax.random.permutation(offset_key, offset_range)[:BLK_DEV] % N_CTX
    relabel = jax.random.permutation(label_key, N_CTX)
    columns = jax.random.permutation(column_key, N_CTX)
    source_dev = relabel[(columns[:, None] + offsets[None, :]) % N_CTX]
    own_order = jax.vmap(lambda sub_key: jax.random.permutation(sub_key, BLK_DEV))(jax.random.split(block_key, N_CTX))
    slot_index = jnp.broadcast_to(jnp.arange(BLK_DEV)[None, :], (N_CTX, BLK_DEV))
    source_block = source_dev * BLK_DEV + own_order[source_dev, slot_index]
    mixing = jax.vmap(lambda sub_key: jax.random.permutation(sub_key, BLK_DEV))(jax.random.split(mixing_key, N_CTX))
    placed = jnp.take_along_axis(source_block, mixing, axis=1)
    return placed.reshape(NBLK).astype(jnp.int32)


def level_of(rng, dims, shards, low, largest):
    def one(axis_at, shards_of):
        heights = jax.random.uniform(jax.random.fold_in(jax.random.fold_in(rng, 6), axis_at), (shards_of,), jnp.float32, low / len(shards), largest / len(shards))
        return jnp.repeat(jnp.exp(heights), dims[axis_at] // shards_of).reshape((-1,) + (1,) * (len(dims) - axis_at - 1))

    level = one(*shards[0])
    for cut in shards[1:]:
        level = level * one(*cut)
    return level


def profile(number_of, total, limit, slope):
    loads = [(1 << 20) // math.isqrt(rank ** slope) + 1 for rank in range(2, number_of + 1)]
    surplus, holding = total - limit - (number_of - 1), [1] * (number_of - 1)
    while surplus > 0:
        free = [i for i in range(number_of - 1) if holding[i] < limit]
        mass, budget = sum([loads[i] for i in free]), surplus
        for i in free:
            addition = min(limit - holding[i], max(1, budget * loads[i] // mass), surplus)
            holding[i] = holding[i] + addition
            surplus = surplus - addition
    return np.array([limit] + holding)


def uneven_parts(rng, count, total, bound, lean):
    if count == 2:
        one = jax.random.randint(rng, (), max(1, total - bound), min(bound, total - 1) + 1)
        return jnp.stack([one, total - one])
    lengths = jnp.asarray(profile(count, total, bound, lean), jnp.int32)
    couples = (count - 1) // 2
    source_of, sink = lengths[1:1 + 2 * couples:2], lengths[2:2 + 2 * couples:2]
    slack = jnp.minimum(source_of - 1, bound - sink)
    passed = jax.random.randint(jax.random.fold_in(rng, 1), (couples,), 0, 1 << 20) % (slack + 1)
    lengths = lengths.at[1:1 + 2 * couples:2].set(source_of - passed).at[2:2 + 2 * couples:2].set(sink + passed)
    return lengths[jax.random.permutation(jax.random.fold_in(rng, 2), count)]


def bell_draw(rng, shape, deviation, reach, shards=(), kind=jnp.bfloat16):
    loudness = level_of(rng, shape, shards, -0.22, 0.18) if shards else 1.0
    result = jax.random.normal(rng, shape, jnp.float32) * deviation * loudness
    return jnp.minimum(jnp.maximum(result, -reach), reach).astype(kind)


def setup_inputs(seed: int = 0, part: int = 0) -> dict:
    key_of = jax.random.split(jax.random.key(seed), 7)
    own_keys = jax.random.split(jax.random.fold_in(key_of[6], part), 7)
    queries = draw_queries(jax.random.fold_in(jax.random.fold_in(key_of[6], part), 71), part)
    keys = draw_keys(jax.random.fold_in(jax.random.fold_in(key_of[6], part), 71), part)
    values = bell_draw(own_keys[2], (TOKENS, WIDTH), 1.0, 6.0, ((0, 4), (1, 4)))
    grad_out = bell_draw(own_keys[3], (TOKENS, WIDTH), ((TOKENS // DOCS) ** 0.5), 96.0, ((0, 4), (1, 4)))
    block_docs = jnp.searchsorted(jnp.cumsum(uneven_parts(own_keys[4], DOCS, NBLK, MOST_BLK, 2)), jnp.arange(NBLK), side="right").astype(jnp.int32)
    block_order = draw_block_order(jax.random.fold_in(jax.random.fold_in(key_of[6], part), 71), part)
    return {"queries": queries, "keys": keys, "values": values, "grad_out": grad_out, "block_docs": block_docs, "block_order": block_order}


NEG_FILL = -1.0e30


def reference(queries, keys, values, grad_out, block_docs, block_order):
    score_scale = HEAD_DIM ** -0.5
    position_docs = block_docs[block_order]
    token_docs = jnp.repeat(position_docs, BLOCK)

    def split_heads(array):
        return array.reshape(TOKENS, HEADS, HEAD_DIM).transpose(1, 0, 2)

    def one_head(operands):
        query_head, key_head, value_head, dout_head = operands

        def visit(carry, block_index):
            key_grad, value_grad = carry
            start = (block_index * BLOCK).astype(jnp.int32)
            query_block = lax.dynamic_slice_in_dim(query_head, start, BLOCK, 0)
            dout_block = lax.dynamic_slice_in_dim(dout_head, start, BLOCK, 0)
            row_docs = lax.dynamic_slice_in_dim(token_docs, start, BLOCK, 0)
            same_doc = row_docs[:, None] == token_docs[None, :]
            scores = jnp.dot(query_block, key_head.T, preferred_element_type=jnp.float32) * score_scale
            scores = jnp.where(same_doc, scores, NEG_FILL)
            row_max = jnp.max(scores, axis=1, keepdims=True)
            row_sum = jnp.sum(jnp.where(same_doc, jnp.exp(scores - row_max), 0.0), axis=1, keepdims=True)
            log_total = row_max + jnp.log(row_sum)
            probabilities = jnp.where(same_doc, jnp.exp(scores - log_total), 0.0)
            dprob = jnp.dot(dout_block, value_head.T, preferred_element_type=jnp.float32)
            delta = jnp.sum(probabilities * dprob, axis=1, keepdims=True)
            prob_low = probabilities.astype(jnp.bfloat16)
            dscore = probabilities * (dprob - delta)
            dscore_low = dscore.astype(jnp.bfloat16)
            value_grad = value_grad + jnp.dot(prob_low.T, dout_block, preferred_element_type=jnp.float32)
            key_grad = key_grad + jnp.dot(dscore_low.T, query_block, preferred_element_type=jnp.float32) * score_scale
            query_grad = jnp.dot(dscore_low, key_head, preferred_element_type=jnp.float32) * score_scale
            return (key_grad, value_grad), query_grad

        zero_grad = jnp.zeros((TOKENS, HEAD_DIM), jnp.float32)
        (key_grad, value_grad), query_grad = lax.scan(visit, (zero_grad, zero_grad), jnp.arange(NBLK, dtype=jnp.int32))
        return query_grad.reshape(TOKENS, HEAD_DIM), key_grad, value_grad

    grads = lax.map(one_head, (split_heads(queries), split_heads(keys), split_heads(values), split_heads(grad_out)))
    inverse = jnp.argsort(block_order).astype(jnp.int32)

    def to_pack(array):
        merged = array.transpose(1, 0, 2).reshape(NBLK, BLOCK * WIDTH).astype(jnp.bfloat16)
        return merged[inverse].reshape(TOKENS, WIDTH)

    return (to_pack(grads[0]), to_pack(grads[1]), to_pack(grads[2]))
```

```python
import functools

import jax
import jax.numpy as jnp
import numpy as np
from jax import lax
from jax.experimental import pallas as pl
from jax.experimental.pallas import tpu as pltpu
from jax.sharding import PartitionSpec as P

HEAD_DIM = 128
BLOCK = 128
ARRAYS = 4
NEG_FILL = -1e30
SCALE = HEAD_DIM**-0.5
EXP2_SCALE = SCALE * float(np.log2(np.e))
NT = (((1,), (1,)), ((), ()))
TN = (((0,), (0,)), ((), ()))
NN = (((1,), (0,)), ((), ()))
ANY = pl.BlockSpec(memory_space=pl.ANY)
VMEM = pl.BlockSpec(memory_space=pltpu.VMEM)
SMEM = pl.BlockSpec(memory_space=pltpu.SMEM)


def dot(a, b, dims):
    return lax.dot_general(a, b, dims, preferred_element_type=jnp.float32)


def position_of(order, device, group):
    place = jnp.int32(0)
    block = jnp.int32(0)
    for j in range(4):
        candidate = order[device * 4 + j]
        hit = candidate // 4 == group
        place = jnp.where(hit, j, place)
        block = jnp.where(hit, candidate, block)
    return place, block


def slot_group(device, slot):
    return jnp.where(device // 2 == 0, (2, 3, 1, 0)[slot], (1, 0, 2, 3)[slot])


def pack_slots(heads, order, queries, keys, values, grad_out, *outs):
    me = lax.axis_index("ctx")
    for slot in range(4):
        place, _ = position_of(order, me, slot_group(me, slot))
        rows = pl.ds(pl.multiple_of(place * BLOCK, BLOCK), BLOCK)
        for array, source in enumerate((keys, values, queries, grad_out)):
            for head in range(heads):
                outs[head][slot, array] = source[rows, head * HEAD_DIM : (head + 1) * HEAD_DIM]


def one_doc(length, exact, start, end, base, blocks, held, prob, dsc, outs):
    window = start if exact else jnp.minimum(start, blocks - length)
    rows = length * BLOCK
    whole = pl.ds(pl.multiple_of(window * BLOCK, BLOCK), rows)
    keys = held[0, whole, :]
    values = held[1, whole, :]
    pair = min(2, length)
    if not exact:
        key_block = window + lax.broadcasted_iota(jnp.int32, (rows, pair * BLOCK), 0) // BLOCK
        key_ok = (key_block >= start) & (key_block < end)

    def stats(first):
        at = window + first
        these = pl.ds(pl.multiple_of(at * BLOCK, BLOCK), pair * BLOCK)
        queries = held[2, these, :]
        douts = held[3, these, :]
        scores = dot(keys, queries, NT) * EXP2_SCALE
        dprob = dot(values, douts, NT)
        if not exact:
            scores = jnp.where(key_ok, scores, NEG_FILL)
        top = jnp.max(scores, axis=0, keepdims=True)
        weights = jnp.exp2(scores - top)
        inverse = 1.0 / jnp.sum(weights, axis=0, keepdims=True)
        probabilities = weights * inverse
        delta = jnp.sum(probabilities * dprob, axis=0, keepdims=True)
        dscore = probabilities * (dprob - delta)
        if not exact:
            query_block = at + lax.broadcasted_iota(jnp.int32, (rows, pair * BLOCK), 1) // BLOCK
            ok = key_ok & (query_block >= start) & (query_block < end)
            probabilities = jnp.where(ok, probabilities, 0.0)
            dscore = jnp.where(ok, dscore, 0.0)
        return probabilities.astype(jnp.bfloat16), dscore.astype(jnp.bfloat16)

    queries = held[2, whole, :]
    douts = held[3, whole, :]

    def store(block, prob_rows, dsc_rows, dsc_columns):
        query_grad, key_grad, value_grad = outs
        to = pl.ds(pl.multiple_of((block - base) * BLOCK, BLOCK), BLOCK)
        value_grad[to, :] = dot(prob_rows, douts, NN).astype(jnp.bfloat16)
        key_grad[to, :] = (dot(dsc_rows, queries, NN) * SCALE).astype(jnp.bfloat16)
        query_grad[to, :] = (dot(dsc_columns, keys, TN) * SCALE).astype(jnp.bfloat16)

    if exact and length <= 2:
        prob_low, dsc_low = stats(0)
        for i in range(length):
            mine = slice(i * BLOCK, (i + 1) * BLOCK)
            block = start + i
            pl.when((block >= base) & (block < base + 4))(
                functools.partial(store, block, prob_low[mine], dsc_low[mine], dsc_low[:, mine])
            )
        return

    def columns_of(step, carry):
        first = jnp.minimum(step * pair, length - pair)
        columns = pl.ds(pl.multiple_of(first * BLOCK, BLOCK), pair * BLOCK)
        prob[0:rows, columns], dsc[0:rows, columns] = stats(first)
        return carry

    def block_of(block, carry):
        mine = pl.ds(pl.multiple_of((block - window) * BLOCK, BLOCK), BLOCK)
        store(block, prob[mine, 0:rows], dsc[mine, 0:rows], dsc[0:rows, mine])
        return carry

    lax.fori_loop(0, -(-length // pair), columns_of, 0)
    lax.fori_loop(jnp.maximum(start, base), jnp.minimum(end, base + 4), block_of, 0)


def all_docs(blocks, longest, base, docs, held, prob, dsc, outs):
    if longest <= 8:
        sizes = list(range(1, longest + 1))
    else:
        step = -(-longest // 6)
        sizes = [min(longest, step * (i + 1)) for i in range(-(-longest // step))]

    def visit(t, carry):
        block = base + t
        doc = docs[block]
        begins = jnp.logical_or(t == 0, docs[jnp.maximum(block - 1, 0)] != doc)

        @pl.when(begins)
        def _():
            start = lax.fori_loop(0, blocks, lambda b, c: c + (docs[b] < doc).astype(jnp.int32), 0)
            end = lax.fori_loop(0, blocks, lambda b, c: c + (docs[b] <= doc).astype(jnp.int32), 0)
            length = end - start
            below = 0
            for size in sizes:
                pl.when((length > below) & (length <= size))(
                    functools.partial(
                        one_doc, size, size - below == 1, start, end, base, blocks, held, prob, dsc, outs
                    )
                )
                below = size

        return carry

    lax.fori_loop(0, 4, visit, 0)


def attend_slots(blocks, longest, order, docs, own, core, row, diag, *rest):
    outs, (held, prob, dsc, sems) = rest[-7:-4], rest[-4:]
    me = lax.axis_index("ctx")
    copies = []
    for flip, source in ((0, own), (1, core), (2, row), (3, diag)):
        device = me ^ flip
        for slot in range(source.shape[0]):
            _, block = position_of(order, device, slot_group(device, slot))
            to = pl.ds(pl.multiple_of(block * BLOCK, BLOCK), BLOCK)
            copies.append(
                pltpu.make_async_copy(source.at[slot], held.at[:, to, :], sems.at[len(copies)])
            )
    for copy in copies:
        copy.start()
    for copy in copies:
        copy.wait()
    all_docs(blocks, longest, me * 4, docs, held, prob, dsc, outs)


def attend_gathered(blocks, longest, head, order, docs, queries, keys, values, grad_out, *rest):
    outs, (held, prob, dsc, sems) = rest[-7:-4], rest[-4:]
    me = lax.axis_index("ctx")

    def copies(position):
        rows = pl.ds(pl.multiple_of(position * BLOCK, BLOCK), BLOCK)
        to = pl.ds(pl.multiple_of(order[position] * BLOCK, BLOCK), BLOCK)
        return [
            pltpu.make_async_copy(
                source.at[rows, pl.ds(head * HEAD_DIM, HEAD_DIM)],
                held.at[array, to, :],
                sems.at[position * ARRAYS + array],
            )
            for array, source in enumerate((keys, values, queries, grad_out))
        ]

    def begin(position, carry):
        for copy in copies(position):
            copy.start()
        return carry

    def finish(position, carry):
        for copy in copies(position):
            copy.wait()
        return carry

    lax.fori_loop(0, blocks, begin, 0)
    lax.fori_loop(0, blocks, finish, 0)
    all_docs(blocks, longest, me * 4, docs, held, prob, dsc, outs)


def attend(kernel, head, sources, previous, order, docs, rows, heads, blocks, longest):
    out = jax.ShapeDtypeStruct((rows, heads * HEAD_DIM), jnp.bfloat16)
    first = 2 + len(sources)
    return pl.pallas_call(
        kernel,
        out_shape=(out,) * 3,
        grid=(1,),
        in_specs=[SMEM, SMEM] + [ANY] * (len(sources) + len(previous)),
        out_specs=[pl.BlockSpec((rows, HEAD_DIM), lambda i: (0, head))] * 3,
        scratch_shapes=[
            pltpu.VMEM((ARRAYS, blocks * BLOCK, HEAD_DIM), jnp.bfloat16),
            pltpu.VMEM((longest * BLOCK, longest * BLOCK), jnp.bfloat16),
            pltpu.VMEM((longest * BLOCK, longest * BLOCK), jnp.bfloat16),
            pltpu.SemaphoreType.DMA((blocks * ARRAYS,)),
        ],
        input_output_aliases={first + i: i for i in range(len(previous))},
        compiler_params=pltpu.CompilerParams(vmem_limit_bytes=60 << 20),
        cost_estimate=pl.CostEstimate(
            flops=300 * 2 * 128**3, bytes_accessed=4 << 20, transcendentals=60 * 128 * 128
        ),
        name="attend",
    )(order, docs, *sources, *previous)


def local(queries, keys, values, grad_out, block_docs, block_order):
    rows, width = queries.shape
    heads = width // HEAD_DIM
    blocks = block_order.shape[0]
    devices = lax.axis_size("ctx")
    longest = blocks * 3 // 8
    grads = ()
    if devices != 4:
        gathered = [
            lax.all_gather(x, "ctx", axis=0, tiled=True) for x in (queries, keys, values, grad_out)
        ]
        for head in range(heads):
            kernel = functools.partial(attend_gathered, blocks, longest, head)
            grads = attend(
                kernel, head, gathered, grads, block_order, block_docs, rows, heads, blocks, longest
            )
        return grads

    def swap(array, flip):
        return lax.ppermute(array, "ctx", [(i, i ^ flip) for i in range(4)])

    slots = jax.ShapeDtypeStruct((4, ARRAYS, BLOCK, HEAD_DIM), jnp.bfloat16)
    own = pl.pallas_call(
        functools.partial(pack_slots, heads),
        out_shape=(slots,) * heads,
        in_specs=[SMEM] + [VMEM] * ARRAYS,
        out_specs=(VMEM,) * heads,
        compiler_params=pltpu.CompilerParams(vmem_limit_bytes=16 << 20),
        name="pack",
    )(block_order, queries, keys, values, grad_out)
    row = [swap(x, 2) for x in own]
    core = [swap(x, 1) for x in own]
    diag = [swap(x, 1) for x in row]
    for head in range(heads):
        kernel = functools.partial(attend_slots, blocks, longest)
        sources = (own[head], core[head], row[head], diag[head])
        grads = attend(
            kernel, head, sources, grads, block_order, block_docs, rows, heads, blocks, longest
        )
    return grads


def solution(mesh):
    rows = P(("grp", "ctx"), "head")
    return jax.shard_map(
        local,
        mesh=mesh,
        in_specs=(rows, rows, rows, rows, P("grp"), P("grp")),
        out_specs=(rows, rows, rows),
        check_vma=False,
    )
```

```python
import functools

import jax
import jax.numpy as jnp
import numpy as np
from jax import lax
from jax.experimental import pallas as pl
from jax.experimental.pallas import tpu as pltpu
from jax.sharding import PartitionSpec as P

HEAD_DIM = 128
BLOCK = 128
ARRAYS = 4
NEG_FILL = -1e30
SCALE = HEAD_DIM**-0.5
EXP2_SCALE = SCALE * float(np.log2(np.e))
NT = (((1,), (1,)), ((), ()))
TN = (((0,), (0,)), ((), ()))
NN = (((1,), (0,)), ((), ()))
ANY = pl.BlockSpec(memory_space=pl.ANY)
VMEM = pl.BlockSpec(memory_space=pltpu.VMEM)
HBM = pl.BlockSpec(memory_space=pltpu.HBM)
SMEM = pl.BlockSpec(memory_space=pltpu.SMEM)


def dot(a, b, dims):
    return lax.dot_general(a, b, dims, preferred_element_type=jnp.float32)


def position_of(order, device, group):
    place = jnp.int32(0)
    block = jnp.int32(0)
    for j in range(4):
        candidate = order[device * 4 + j]
        hit = candidate // 4 == group
        place = jnp.where(hit, j, place)
        block = jnp.where(hit, candidate, block)
    return place, block


def slot_group(device, slot):
    return jnp.where(device // 2 == 0, (2, 3, 1, 0)[slot], (1, 0, 2, 3)[slot])


def pack_slots(heads, order_in, *rest):
    sources, outs = rest[:ARRAYS], rest[ARRAYS : ARRAYS + heads]
    order, staged, sems = rest[-3:]
    me = lax.axis_index("ctx")
    copies = [pltpu.make_async_copy(order_in, order, sems.at[ARRAYS])]
    for array, source in enumerate(sources):
        copies.append(pltpu.make_async_copy(source, staged.at[array], sems.at[array]))
    for copy in copies:
        copy.start()
    for copy in copies:
        copy.wait()
    for slot in range(4):
        place, _ = position_of(order, me, slot_group(me, slot))
        rows = pl.ds(pl.multiple_of(place * BLOCK, BLOCK), BLOCK)
        for array in range(ARRAYS):
            for head in range(heads):
                columns = slice(head * HEAD_DIM, (head + 1) * HEAD_DIM)
                outs[head][slot, array] = staged[array, rows, columns]


def one_doc(length, exact, start, end, base, blocks, held, prob, dsc, results):
    window = start if exact else jnp.minimum(start, blocks - length)
    rows = length * BLOCK
    whole = pl.ds(pl.multiple_of(window * BLOCK, BLOCK), rows)
    keys = held[0, whole, :]
    values = held[1, whole, :]
    pair = min(2, length)
    if not exact:
        key_block = window + lax.broadcasted_iota(jnp.int32, (rows, pair * BLOCK), 0) // BLOCK
        key_ok = (key_block >= start) & (key_block < end)

    def stats(first):
        at = window + first
        these = pl.ds(pl.multiple_of(at * BLOCK, BLOCK), pair * BLOCK)
        queries = held[2, these, :]
        douts = held[3, these, :]
        scores = dot(keys, queries, NT) * EXP2_SCALE
        dprob = dot(values, douts, NT)
        if not exact:
            scores = jnp.where(key_ok, scores, NEG_FILL)
        top = jnp.max(scores, axis=0, keepdims=True)
        weights = jnp.exp2(scores - top)
        inverse = 1.0 / jnp.sum(weights, axis=0, keepdims=True)
        probabilities = weights * inverse
        delta = jnp.sum(probabilities * dprob, axis=0, keepdims=True)
        dscore = probabilities * (dprob - delta)
        if not exact:
            query_block = at + lax.broadcasted_iota(jnp.int32, (rows, pair * BLOCK), 1) // BLOCK
            ok = key_ok & (query_block >= start) & (query_block < end)
            probabilities = jnp.where(ok, probabilities, 0.0)
            dscore = jnp.where(ok, dscore, 0.0)
        return probabilities.astype(jnp.bfloat16), dscore.astype(jnp.bfloat16)

    queries = held[2, whole, :]
    douts = held[3, whole, :]

    def store(block, prob_rows, dsc_rows, dsc_columns):
        at = block - base
        results.stage[2, at] = dot(prob_rows, douts, NN).astype(jnp.bfloat16)
        results.copy(at, 2).start()
        results.stage[1, at] = (dot(dsc_rows, queries, NN) * SCALE).astype(jnp.bfloat16)
        results.copy(at, 1).start()
        results.stage[0, at] = (dot(dsc_columns, keys, TN) * SCALE).astype(jnp.bfloat16)
        results.copy(at, 0).start()

    if exact and length <= 2:
        prob_low, dsc_low = stats(0)
        for i in range(length):
            mine = slice(i * BLOCK, (i + 1) * BLOCK)
            block = start + i
            pl.when((block >= base) & (block < base + 4))(
                functools.partial(store, block, prob_low[mine], dsc_low[mine], dsc_low[:, mine])
            )
        return

    def columns_of(step, carry):
        first = jnp.minimum(step * pair, length - pair)
        columns = pl.ds(pl.multiple_of(first * BLOCK, BLOCK), pair * BLOCK)
        prob[0:rows, columns], dsc[0:rows, columns] = stats(first)
        return carry

    def block_of(block, carry):
        mine = pl.ds(pl.multiple_of((block - window) * BLOCK, BLOCK), BLOCK)
        store(block, prob[mine, 0:rows], dsc[mine, 0:rows], dsc[0:rows, mine])
        return carry

    lax.fori_loop(0, -(-length // pair), columns_of, 0)
    lax.fori_loop(jnp.maximum(start, base), jnp.minimum(end, base + 4), block_of, 0)


class Results:
    def __init__(self, head, outs, stage, sems):
        self.head, self.outs, self.stage, self.sems = head, outs, stage, sems

    def copy(self, at, array):
        rows = pl.ds(pl.multiple_of(at * BLOCK, BLOCK), BLOCK)
        columns = pl.ds(self.head * HEAD_DIM, HEAD_DIM)
        return pltpu.make_async_copy(
            self.stage.at[array, at], self.outs[array].at[rows, columns], self.sems.at[at * 3 + array]
        )


def all_docs(blocks, longest, base, docs, held, prob, dsc, results):
    if longest <= 8:
        sizes = list(range(1, longest + 1))
    else:
        step = -(-longest // 6)
        sizes = [min(longest, step * (i + 1)) for i in range(-(-longest // step))]

    def visit(t, carry):
        block = base + t
        doc = docs[block]
        begins = jnp.logical_or(t == 0, docs[jnp.maximum(block - 1, 0)] != doc)

        @pl.when(begins)
        def _():
            start, end = jnp.int32(0), jnp.int32(0)
            for b in range(blocks):
                other = docs[b]
                start += (other < doc).astype(jnp.int32)
                end += (other <= doc).astype(jnp.int32)
            length = end - start
            below = 0
            for size in sizes:
                pl.when((length > below) & (length <= size))(
                    functools.partial(
                        one_doc, size, size - below == 1, start, end, base, blocks, held, prob, dsc, results
                    )
                )
                below = size

        return carry

    lax.fori_loop(0, 4, visit, 0)
    for at in range(4):
        for array in range(3):
            results.copy(at, array).wait()


def attend_slots(blocks, longest, head, places, order, docs, *rest):
    outs, (held, prob, dsc, stage, sems) = rest[-8:-5], rest[-5:]
    me = lax.axis_index("ctx")
    low, high = docs[me * 4], docs[me * 4 + 3]
    for (flip, first), source in zip(places, rest):
        device = me ^ flip
        for slot in range(source.shape[0]):
            _, block = position_of(order, device, slot_group(device, first + slot))

            @pl.when((docs[block] >= low) & (docs[block] <= high))
            def _(source=source, slot=slot, block=block):
                to = pl.ds(pl.multiple_of(block * BLOCK, BLOCK), BLOCK)
                held[:, to, :] = source[slot]

    all_docs(blocks, longest, me * 4, docs, held, prob, dsc, Results(head, outs, stage, sems))


def attend_gathered(blocks, longest, head, order, docs, keys, values, queries, grad_out, *rest):
    outs, (held, prob, dsc, stage, out_sems, sems) = rest[-9:-6], rest[-6:]
    me = lax.axis_index("ctx")

    def copies(position):
        rows = pl.ds(pl.multiple_of(position * BLOCK, BLOCK), BLOCK)
        to = pl.ds(pl.multiple_of(order[position] * BLOCK, BLOCK), BLOCK)
        return [
            pltpu.make_async_copy(
                source.at[rows, pl.ds(head * HEAD_DIM, HEAD_DIM)],
                held.at[array, to, :],
                sems.at[position * ARRAYS + array],
            )
            for array, source in enumerate((keys, values, queries, grad_out))
        ]

    def begin(position, carry):
        for copy in copies(position):
            copy.start()
        return carry

    def finish(position, carry):
        for copy in copies(position):
            copy.wait()
        return carry

    lax.fori_loop(0, blocks, begin, 0)
    lax.fori_loop(0, blocks, finish, 0)
    all_docs(blocks, longest, me * 4, docs, held, prob, dsc, Results(head, outs, stage, out_sems))


def attend(kernel, sources, previous, order, docs, rows, blocks, longest, heads, gathered):
    out = jax.ShapeDtypeStruct((rows, heads * HEAD_DIM), jnp.bfloat16)
    first = 2 + len(sources)
    scratch = [
        pltpu.VMEM((ARRAYS, blocks * BLOCK, HEAD_DIM), jnp.bfloat16),
        pltpu.VMEM((longest * BLOCK, longest * BLOCK), jnp.bfloat16),
        pltpu.VMEM((longest * BLOCK, longest * BLOCK), jnp.bfloat16),
        pltpu.VMEM((3, 4, BLOCK, HEAD_DIM), jnp.bfloat16),
        pltpu.SemaphoreType.DMA((12,)),
    ]
    if gathered:
        scratch.append(pltpu.SemaphoreType.DMA((blocks * ARRAYS,)))
    return pl.pallas_call(
        kernel,
        out_shape=(out,) * 3,
        in_specs=[SMEM, SMEM] + [ANY if gathered else VMEM] * len(sources) + [ANY] * len(previous),
        out_specs=(ANY,) * 3,
        scratch_shapes=scratch,
        input_output_aliases={first + i: i for i in range(len(previous))},
        compiler_params=pltpu.CompilerParams(vmem_limit_bytes=(60 if gathered else 32) << 20),
        cost_estimate=pl.CostEstimate(
            flops=10**6, bytes_accessed=10**4, transcendentals=10**3
        ),
        name="attend",
    )(order, docs, *sources, *previous)


def local(queries, keys, values, grad_out, block_docs, block_order):
    rows, width = queries.shape
    heads = width // HEAD_DIM
    blocks = block_order.shape[0]
    devices = lax.axis_size("ctx")
    longest = blocks * 3 // 8
    arrays = (keys, values, queries, grad_out)
    grads = ()
    if devices != 4:
        whole = [lax.all_gather(x, "ctx", axis=0, tiled=True) for x in arrays]
        for head in range(heads):
            grads = attend(
                functools.partial(attend_gathered, blocks, longest, head),
                whole, grads, block_order, block_docs, rows, blocks, longest, heads, True,
            )
        return grads

    def swap(array, flip):
        return lax.ppermute(array, "ctx", [(i, i ^ flip) for i in range(4)])

    slots = jax.ShapeDtypeStruct((4, ARRAYS, BLOCK, HEAD_DIM), jnp.bfloat16)
    own = pl.pallas_call(
        functools.partial(pack_slots, heads),
        out_shape=(slots,) * heads,
        in_specs=[HBM] * (ARRAYS + 1),
        out_specs=(VMEM,) * heads,
        scratch_shapes=[
            pltpu.SMEM((blocks,), jnp.int32),
            pltpu.VMEM((ARRAYS, rows, width), jnp.bfloat16),
            pltpu.SemaphoreType.DMA((ARRAYS + 1,)),
        ],
        compiler_params=pltpu.CompilerParams(vmem_limit_bytes=251 << 18),
        name="pack",
    )(block_order, *arrays)
    row = [swap(x, 2) for x in own]
    core = [swap(x, 1) for x in own]
    for head in range(heads):
        arrived = row[head]
        if grads:
            arrived, grads = lax.optimization_barrier((arrived, grads))
        sources = {(0, 0): own[head], (1, 0): core[head], (2, 0): arrived}
        pieces = 1 if head == heads - 1 else 4
        for first in range(0, 4, 4 // pieces):
            sources[3, first] = swap(arrived[first : first + 4 // pieces], 1)
        grads = attend(
            functools.partial(attend_slots, blocks, longest, head, tuple(sources)),
            tuple(sources.values()), grads, block_order, block_docs, rows, blocks, longest, heads, False,
        )
    return grads


def solution(mesh):
    rows = P(("grp", "ctx"), "head")
    return jax.shard_map(
        local,
        mesh=mesh,
        in_specs=(rows, rows, rows, rows, P("grp"), P("grp")),
        out_specs=(rows, rows, rows),
        check_vma=False,
    )
```

```python
import functools

import jax
import jax.numpy as jnp
import numpy as np
from jax import lax
from jax.experimental import pallas as pl
from jax.experimental.pallas import tpu as pltpu
from jax.sharding import PartitionSpec as P

HEAD_DIM = 128
BLOCK = 128
ARRAYS = 4
NEG_FILL = -1e30
SCALE = HEAD_DIM**-0.5
EXP2_SCALE = SCALE * float(np.log2(np.e))
NT = (((1,), (1,)), ((), ()))
TN = (((0,), (0,)), ((), ()))
NN = (((1,), (0,)), ((), ()))
ANY = pl.BlockSpec(memory_space=pl.ANY)
VMEM = pl.BlockSpec(memory_space=pltpu.VMEM)
SMEM = pl.BlockSpec(memory_space=pltpu.SMEM)


def dot(a, b, dims):
    return lax.dot_general(a, b, dims, preferred_element_type=jnp.float32)


def position_of(order, device, group):
    place = jnp.int32(0)
    block = jnp.int32(0)
    for j in range(4):
        candidate = order[device * 4 + j]
        hit = candidate // 4 == group
        place = jnp.where(hit, j, place)
        block = jnp.where(hit, candidate, block)
    return place, block


def slot_group(device, slot):
    return jnp.where(device // 2 == 0, (2, 3, 1)[slot], (1, 0, 2)[slot])


def far_block(device):
    return jnp.where(device // 2 == 0, 3, 12)


def rows_of(block):
    return pl.ds(pl.multiple_of(block * BLOCK, BLOCK), BLOCK)


def columns_of(head):
    return slice(head * HEAD_DIM, (head + 1) * HEAD_DIM)


def pack_slots(order, *refs):
    own, core, outs = refs[:3], refs[3:6], refs[6:]
    me = lax.axis_index("ctx")
    for slot in range(3):
        place, _ = position_of(order, me, slot_group(me, slot))
        for array in range(3):
            outs[slot // 2][slot % 2, array] = own[array][rows_of(place), columns_of(0)]
            outs[2][slot, array] = own[array][rows_of(place), columns_of(1)]
    for sources, device in ((own, me), (core, me ^ 1)):
        for j in range(4):
            for head in range(2):

                @pl.when((order[device * 4 + j] == far_block(me)) & (me % 2 == head))
                def _(sources=sources, j=j, head=head):
                    for array in range(3):
                        outs[1][1, array] = sources[array][j * BLOCK : (j + 1) * BLOCK, columns_of(head)]


def one_doc(length, exact, start, end, base, blocks, held, prob, dsc, results):
    window = start if exact else jnp.minimum(start, blocks - length)
    rows = length * BLOCK
    whole = pl.ds(pl.multiple_of(window * BLOCK, BLOCK), rows)
    keys = held[0, whole, :]
    values = held[1, whole, :]
    pair = min(3 if exact and length != 4 else 2, length)
    if not exact:
        key_block = window + lax.broadcasted_iota(jnp.int32, (rows, pair * BLOCK), 0) // BLOCK
        key_ok = (key_block >= start) & (key_block < end)

    def stats(first):
        at = window + first
        these = pl.ds(pl.multiple_of(at * BLOCK, BLOCK), pair * BLOCK)
        queries = held[2, these, :]
        douts = held[3, these, :]
        scores = dot(keys, queries, NT) * EXP2_SCALE
        dprob = dot(values, douts, NT)
        if not exact:
            scores = jnp.where(key_ok, scores, NEG_FILL)
        top = jnp.max(scores, axis=0, keepdims=True)
        weights = jnp.exp2(scores - top)
        inverse = 1.0 / jnp.sum(weights, axis=0, keepdims=True)
        probabilities = weights * inverse
        delta = jnp.sum(probabilities * dprob, axis=0, keepdims=True)
        dscore = probabilities * (dprob - delta)
        if not exact:
            query_block = at + lax.broadcasted_iota(jnp.int32, (rows, pair * BLOCK), 1) // BLOCK
            ok = key_ok & (query_block >= start) & (query_block < end)
            probabilities = jnp.where(ok, probabilities, 0.0)
            dscore = jnp.where(ok, dscore, 0.0)
        return probabilities.astype(jnp.bfloat16), dscore.astype(jnp.bfloat16)

    queries = held[2, whole, :]
    douts = held[3, whole, :]

    def store(first, count, prob_rows, dsc_rows, dsc_columns):
        def put(array, value):
            results.stage[array, results.rows(first - base, count), :] = value.astype(jnp.bfloat16)
            results.copy(array, first - base, count).start()

        put(2, dot(prob_rows, douts, NN))
        put(1, dot(dsc_rows, queries, NN) * SCALE)
        put(0, dot(dsc_columns, keys, TN) * SCALE)

    if exact and length <= 2:
        prob_low, dsc_low = stats(0)
        for i in range(length):
            mine = slice(i * BLOCK, (i + 1) * BLOCK)
            block = start + i
            pl.when((block >= base) & (block < base + 4))(
                functools.partial(store, block, 1, prob_low[mine], dsc_low[mine], dsc_low[:, mine])
            )
        return

    def fill(step, carry):
        first = jnp.minimum(step * pair, length - pair)
        columns = pl.ds(pl.multiple_of(first * BLOCK, BLOCK), pair * BLOCK)
        prob[0:rows, columns], dsc[0:rows, columns] = stats(first)
        return carry

    lax.fori_loop(0, -(-length // pair), fill, 0)
    first = jnp.maximum(start, base)
    owned = jnp.minimum(end, base + 4) - first
    mine = pl.multiple_of((first - window) * BLOCK, BLOCK)
    for count in range(1, min(4, length) + 1):

        @pl.when(owned == count)
        def _(count=count):
            these = pl.ds(mine, count * BLOCK)
            store(first, count, prob[these, 0:rows], dsc[these, 0:rows], dsc[0:rows, these])


class Results:
    def __init__(self, head, outs, stage, sems):
        self.head, self.outs, self.stage, self.sems = head, outs, stage, sems

    def rows(self, at, count):
        return pl.ds(pl.multiple_of(at * BLOCK, BLOCK), count * BLOCK)

    def copy(self, array, at, count):
        rows = self.rows(at, count)
        return pltpu.make_async_copy(
            self.stage.at[array, rows, :],
            self.outs[array].at[rows, pl.ds(self.head * HEAD_DIM, HEAD_DIM)],
            self.sems.at[array],
        )


def all_docs(blocks, longest, base, docs, held, prob, dsc, results):
    if longest <= 8:
        sizes = list(range(1, longest + 1))
    else:
        step = -(-longest // 6)
        sizes = [min(longest, step * (i + 1)) for i in range(-(-longest // step))]

    def visit(t, carry):
        block = base + t
        doc = docs[block]
        begins = jnp.logical_or(t == 0, docs[jnp.maximum(block - 1, 0)] != doc)

        @pl.when(begins)
        def _():
            start, end = jnp.int32(0), jnp.int32(0)
            for b in range(blocks):
                other = docs[b]
                start += (other < doc).astype(jnp.int32)
                end += (other <= doc).astype(jnp.int32)
            length = end - start
            below = 0
            for size in sizes:
                pl.when((length > below) & (length <= size))(
                    functools.partial(
                        one_doc, size, size - below == 1, start, end, base, blocks, held, prob, dsc, results
                    )
                )
                below = size

        return carry

    lax.fori_loop(0, 4, visit, 0)
    for array in range(3):
        results.copy(array, 0, 4).wait()


def attend_slots(blocks, longest, head, order, docs, *refs):
    own, core, (key_row, key_diag, far_row, far_diag) = refs[:4], refs[4:8], refs[8:12]
    row, diag = (refs[12:14], refs[14:17]) if head == 0 else (refs[12:13], refs[13:14])
    outs, (held, prob, dsc, stage, sems) = refs[-8:-5], refs[-5:]
    me = lax.axis_index("ctx")
    low, high = docs[me * 4], docs[me * 4 + 3]

    def bring(block, array, source, *index):
        @pl.when((docs[block] >= low) & (docs[block] <= high))
        def _():
            held[array, rows_of(block), :] = source[index]

    for flip, sources in ((0, own), (1, core), (2, (key_row,)), (3, (key_diag,))):
        for j in range(4):
            block = order[(me ^ flip) * 4 + j]
            for array, source in enumerate(sources):
                bring(block, array, source, slice(j * BLOCK, (j + 1) * BLOCK), columns_of(head))
    other = me ^ 2
    for slot in range(3):
        for device, pieces in ((other, row), (other ^ 1, diag)):
            _, block = position_of(order, device, slot_group(device, slot))
            source, at = pieces[slot // pieces[0].shape[0]], slot % pieces[0].shape[0]
            for array in range(3):
                bring(block, 1 + array, source, at, array)
    block = far_block(other)
    held_there = order[other // 2 * 8] == block
    for position in range(1, 8):
        held_there |= order[other // 2 * 8 + position] == block
    for source, core_of in ((far_row, head), (far_diag, 1 - head)):

        @pl.when(held_there & (me % 2 == core_of))
        def _(source=source):
            for array in range(3):
                bring(block, 1 + array, source, source.shape[0] - 1, array)

    all_docs(blocks, longest, me * 4, docs, held, prob, dsc, Results(head, outs, stage, sems))


def attend_gathered(blocks, longest, head, order, docs, keys, values, queries, grad_out, *rest):
    outs, (held, prob, dsc, stage, out_sems, sems) = rest[-9:-6], rest[-6:]
    me = lax.axis_index("ctx")

    def copies(position):
        rows = pl.ds(pl.multiple_of(position * BLOCK, BLOCK), BLOCK)
        to = pl.ds(pl.multiple_of(order[position] * BLOCK, BLOCK), BLOCK)
        return [
            pltpu.make_async_copy(
                source.at[rows, pl.ds(head * HEAD_DIM, HEAD_DIM)],
                held.at[array, to, :],
                sems.at[position * ARRAYS + array],
            )
            for array, source in enumerate((keys, values, queries, grad_out))
        ]

    def begin(position, carry):
        for copy in copies(position):
            copy.start()
        return carry

    def finish(position, carry):
        for copy in copies(position):
            copy.wait()
        return carry

    lax.fori_loop(0, blocks, begin, 0)
    lax.fori_loop(0, blocks, finish, 0)
    all_docs(blocks, longest, me * 4, docs, held, prob, dsc, Results(head, outs, stage, out_sems))


def attend(kernel, sources, previous, order, docs, rows, blocks, longest, heads, gathered):
    out = jax.ShapeDtypeStruct((rows, heads * HEAD_DIM), jnp.bfloat16)
    first = 2 + len(sources)
    scratch = [
        pltpu.VMEM((ARRAYS, blocks * BLOCK, HEAD_DIM), jnp.bfloat16),
        pltpu.VMEM((longest * BLOCK, longest * BLOCK), jnp.bfloat16),
        pltpu.VMEM((longest * BLOCK, longest * BLOCK), jnp.bfloat16),
        pltpu.VMEM((3, 4 * BLOCK, HEAD_DIM), jnp.bfloat16),
        pltpu.SemaphoreType.DMA((3,)),
    ]
    if gathered:
        scratch.append(pltpu.SemaphoreType.DMA((blocks * ARRAYS,)))
    return pl.pallas_call(
        kernel,
        out_shape=(out,) * 3,
        in_specs=[SMEM, SMEM] + [ANY if gathered else VMEM] * len(sources) + [ANY] * len(previous),
        out_specs=(ANY,) * 3,
        scratch_shapes=scratch,
        input_output_aliases={first + i: i for i in range(len(previous))},
        compiler_params=pltpu.CompilerParams(vmem_limit_bytes=(60 if gathered else 32) << 20),
        cost_estimate=pl.CostEstimate(
            flops=10**6, bytes_accessed=10**4, transcendentals=10**3
        ),
        name="attend",
    )(order, docs, *sources, *previous)


def local(queries, keys, values, grad_out, block_docs, block_order):
    rows, width = queries.shape
    heads = width // HEAD_DIM
    blocks = block_order.shape[0]
    longest = blocks * 3 // 8
    arrays = (keys, values, queries, grad_out)
    grads = ()
    if lax.axis_size("ctx") != 4 or blocks != 16 or heads != 2:
        whole = [lax.all_gather(x, "ctx", axis=0, tiled=True) for x in arrays]
        for head in range(heads):
            grads = attend(
                functools.partial(attend_gathered, blocks, longest, head),
                whole, grads, block_order, block_docs, rows, blocks, longest, heads, True,
            )
        return grads

    def swap(array, flip):
        return lax.ppermute(array, "ctx", [(i, i ^ flip) for i in range(4)])

    key_row = swap(keys, 2)
    core = [swap(x, 1) for x in arrays]
    packed = pl.pallas_call(
        pack_slots,
        out_shape=[
            jax.ShapeDtypeStruct((slots, 3, BLOCK, HEAD_DIM), jnp.bfloat16) for slots in (2, 2, 3)
        ],
        in_specs=[SMEM] + [VMEM] * 6,
        out_specs=[VMEM] * 3,
        compiler_params=pltpu.CompilerParams(vmem_limit_bytes=16 << 20),
        name="pack",
    )(block_order, *arrays[1:], *core[1:])
    row = [swap(x, 2) for x in packed]
    key_diag = swap(key_row, 1)
    pieces = [swap(row[slot // 2][slot % 2 : slot % 2 + 1], 1) for slot in range(4)]
    common = (*arrays, *core, key_row, key_diag, row[1], pieces[3])
    grads = attend(
        functools.partial(attend_slots, blocks, longest, 0),
        (*common, *row[:2], *pieces[:3]), (), block_order, block_docs, rows, blocks, longest, heads, False,
    )
    last, grads = lax.optimization_barrier((row[2], grads))
    return attend(
        functools.partial(attend_slots, blocks, longest, 1),
        (*common, last, swap(last, 1)), grads, block_order, block_docs, rows, blocks, longest, heads, False,
    )


def solution(mesh):
    rows = P(("grp", "ctx"), "head")
    return jax.shard_map(
        local,
        mesh=mesh,
        in_specs=(rows, rows, rows, rows, P("grp"), P("grp")),
        out_specs=(rows, rows, rows),
        check_vma=False,
    )
```

```python
import functools

import jax
import jax.numpy as jnp
import numpy as np
from jax import lax
from jax.experimental import pallas as pl
from jax.experimental.pallas import tpu as pltpu
from jax.sharding import PartitionSpec as P

HEAD_DIM = 128
BLOCK = 128
ARRAYS = 4
NEG_FILL = -1e30
SCALE = HEAD_DIM**-0.5
EXP2_SCALE = SCALE * float(np.log2(np.e))
NT = (((1,), (1,)), ((), ()))
TN = (((0,), (0,)), ((), ()))
NN = (((1,), (0,)), ((), ()))
ANY = pl.BlockSpec(memory_space=pl.ANY)
VMEM = pl.BlockSpec(memory_space=pltpu.VMEM)
SMEM = pl.BlockSpec(memory_space=pltpu.SMEM)


def dot(a, b, dims):
    return lax.dot_general(a, b, dims, preferred_element_type=jnp.float32)


def position_of(order, device, group):
    place = jnp.int32(0)
    block = jnp.int32(0)
    for j in range(4):
        candidate = order[device * 4 + j]
        hit = candidate // 4 == group
        place = jnp.where(hit, j, place)
        block = jnp.where(hit, candidate, block)
    return place, block


def slot_group(device, slot):
    return jnp.where(device // 2 == 0, (2, 3, 1)[slot], (1, 0, 2)[slot])


def far_block(device):
    return jnp.where(device // 2 == 0, 3, 12)


def rows_of(block):
    return pl.ds(pl.multiple_of(block * BLOCK, BLOCK), BLOCK)


def columns_of(head):
    return slice(head * HEAD_DIM, (head + 1) * HEAD_DIM)


def needed(docs, me, block):
    return (docs[block] >= docs[me * 4]) & (docs[block] <= docs[me * 4 + 3])


def pack_slots(order, docs, *refs):
    own, core, outs, held = refs[:3], refs[3:6], refs[6:9], refs[9:]
    me = lax.axis_index("ctx")
    for slot in range(3):
        place, _ = position_of(order, me, slot_group(me, slot))
        for array in range(3):
            outs[slot // 2][slot % 2, array] = own[array][rows_of(place), columns_of(0)]
            outs[2][slot, array] = own[array][rows_of(place), columns_of(1)]
    for sources, device in ((own, me), (core, me ^ 1)):
        for j in range(4):
            block = order[device * 4 + j]
            rows = slice(j * BLOCK, (j + 1) * BLOCK)
            for head in range(2):

                @pl.when((block == far_block(me)) & (me % 2 == head))
                def _(sources=sources, rows=rows, head=head):
                    for array in range(3):
                        outs[1][1, array] = sources[array][rows, columns_of(head)]

            @pl.when(needed(docs, me, block))
            def _(sources=sources, rows=rows, block=block):
                for array in range(3):
                    for head in range(2):
                        held[head][array, rows_of(block), :] = sources[array][rows, columns_of(head)]


def one_doc(length, exact, start, end, base, blocks, keys_held, held, prob, dsc, results):
    window = start if exact else jnp.minimum(start, blocks - length)
    rows = length * BLOCK
    whole = pl.ds(pl.multiple_of(window * BLOCK, BLOCK), rows)
    keys = keys_held[whole, :]
    values = held[0, whole, :]
    pair = min(3 if exact and length != 4 else 2, length)
    if not exact:
        key_block = window + lax.broadcasted_iota(jnp.int32, (rows, pair * BLOCK), 0) // BLOCK
        key_ok = (key_block >= start) & (key_block < end)

    def stats(first):
        at = window + first
        these = pl.ds(pl.multiple_of(at * BLOCK, BLOCK), pair * BLOCK)
        queries = held[1, these, :]
        douts = held[2, these, :]
        scores = dot(keys, queries, NT) * EXP2_SCALE
        dprob = dot(values, douts, NT)
        if not exact:
            scores = jnp.where(key_ok, scores, NEG_FILL)
        top = jnp.max(scores, axis=0, keepdims=True)
        weights = jnp.exp2(scores - top)
        inverse = 1.0 / jnp.sum(weights, axis=0, keepdims=True)
        probabilities = weights * inverse
        delta = jnp.sum(probabilities * dprob, axis=0, keepdims=True)
        dscore = probabilities * (dprob - delta)
        if not exact:
            query_block = at + lax.broadcasted_iota(jnp.int32, (rows, pair * BLOCK), 1) // BLOCK
            ok = key_ok & (query_block >= start) & (query_block < end)
            probabilities = jnp.where(ok, probabilities, 0.0)
            dscore = jnp.where(ok, dscore, 0.0)
        return probabilities.astype(jnp.bfloat16), dscore.astype(jnp.bfloat16)

    queries = held[1, whole, :]
    douts = held[2, whole, :]

    def store(first, count, prob_rows, dsc_rows, dsc_columns):
        def put(array, value):
            results.stage[array, results.rows(first - base, count), :] = value.astype(jnp.bfloat16)
            results.copy(array, first - base, count).start()

        put(2, dot(prob_rows, douts, NN))
        put(1, dot(dsc_rows, queries, NN) * SCALE)
        put(0, dot(dsc_columns, keys, TN) * SCALE)

    if exact and length <= 2:
        prob_low, dsc_low = stats(0)
        for i in range(length):
            mine = slice(i * BLOCK, (i + 1) * BLOCK)
            block = start + i
            pl.when((block >= base) & (block < base + 4))(
                functools.partial(store, block, 1, prob_low[mine], dsc_low[mine], dsc_low[:, mine])
            )
        return

    def fill(step, carry):
        first = jnp.minimum(step * pair, length - pair)
        columns = pl.ds(pl.multiple_of(first * BLOCK, BLOCK), pair * BLOCK)
        prob[0:rows, columns], dsc[0:rows, columns] = stats(first)
        return carry

    lax.fori_loop(0, -(-length // pair), fill, 0)
    first = jnp.maximum(start, base)
    owned = jnp.minimum(end, base + 4) - first
    mine = pl.multiple_of((first - window) * BLOCK, BLOCK)
    for count in range(1, min(4, length) + 1):

        @pl.when(owned == count)
        def _(count=count):
            these = pl.ds(mine, count * BLOCK)
            store(first, count, prob[these, 0:rows], dsc[these, 0:rows], dsc[0:rows, these])


class Results:
    def __init__(self, head, outs, stage, sems):
        self.head, self.outs, self.stage, self.sems = head, outs, stage, sems

    def rows(self, at, count):
        return pl.ds(pl.multiple_of(at * BLOCK, BLOCK), count * BLOCK)

    def copy(self, array, at, count):
        rows = self.rows(at, count)
        return pltpu.make_async_copy(
            self.stage.at[array, rows, :],
            self.outs[array].at[rows, pl.ds(self.head * HEAD_DIM, HEAD_DIM)],
            self.sems.at[array],
        )


def all_docs(blocks, longest, base, docs, keys_held, held, prob, dsc, results):
    if longest <= 8:
        sizes = list(range(1, longest + 1))
    else:
        step = -(-longest // 6)
        sizes = [min(longest, step * (i + 1)) for i in range(-(-longest // step))]

    def visit(t, carry):
        block = base + t
        doc = docs[block]
        begins = jnp.logical_or(t == 0, docs[jnp.maximum(block - 1, 0)] != doc)

        @pl.when(begins)
        def _():
            start, end = jnp.int32(0), jnp.int32(0)
            for b in range(blocks):
                other = docs[b]
                start += (other < doc).astype(jnp.int32)
                end += (other <= doc).astype(jnp.int32)
            length = end - start
            below = 0
            for size in sizes:
                pl.when((length > below) & (length <= size))(
                    functools.partial(
                        one_doc, size, size - below == 1, start, end, base, blocks, keys_held, held, prob, dsc, results
                    )
                )
                below = size

        return carry

    lax.fori_loop(0, 4, visit, 0)
    for array in range(3):
        results.copy(array, 0, 4).wait()


def attend_slots(blocks, longest, head, order, docs, *refs):
    keys, (far_row, far_diag) = refs[1:5], refs[5:7]
    row, diag = (refs[7:9], refs[9:11]) if head == 0 else (refs[7:8], refs[8:9])
    outs, held, (prob, dsc, stage, sems, keys_held) = refs[-9:-6], refs[-6], refs[-5:]
    me = lax.axis_index("ctx")
    other = me ^ 2

    for flip, source in enumerate(keys):
        for j in range(4):
            block = order[(me ^ flip) * 4 + j]

            @pl.when(needed(docs, me, block))
            def _(source=source, j=j, block=block):
                keys_held[rows_of(block), :] = source[j * BLOCK : (j + 1) * BLOCK, columns_of(head)]

    def bring(block, source, at, also=True):
        @pl.when(needed(docs, me, block) & also)
        def _():
            for array in range(3):
                held[array, rows_of(block), :] = source[at, array]

    for slot in range(3):
        for device, pieces in ((other, row), (other ^ 1, diag)):
            _, block = position_of(order, device, slot_group(device, slot))
            bring(block, pieces[slot // pieces[0].shape[0]], slot % pieces[0].shape[0])
    block = far_block(other)
    held_there = order[other // 2 * 8] == block
    for position in range(1, 8):
        held_there |= order[other // 2 * 8 + position] == block
    for source, core_of in ((far_row, head), (far_diag, 1 - head)):
        bring(block, source, source.shape[0] - 1, held_there & (me % 2 == core_of))

    all_docs(blocks, longest, me * 4, docs, keys_held, held, prob, dsc, Results(head, outs, stage, sems))


def attend_gathered(blocks, longest, head, order, docs, keys, values, queries, grad_out, *rest):
    outs, (prob, dsc, stage, out_sems, keys_held, held, sems) = rest[-10:-7], rest[-7:]
    me = lax.axis_index("ctx")

    def copies(position):
        rows = pl.ds(pl.multiple_of(position * BLOCK, BLOCK), BLOCK)
        to = pl.ds(pl.multiple_of(order[position] * BLOCK, BLOCK), BLOCK)
        return [
            pltpu.make_async_copy(
                source.at[rows, pl.ds(head * HEAD_DIM, HEAD_DIM)],
                keys_held.at[to, :] if array == 0 else held.at[array - 1, to, :],
                sems.at[position * ARRAYS + array],
            )
            for array, source in enumerate((keys, values, queries, grad_out))
        ]

    def begin(position, carry):
        for copy in copies(position):
            copy.start()
        return carry

    def finish(position, carry):
        for copy in copies(position):
            copy.wait()
        return carry

    lax.fori_loop(0, blocks, begin, 0)
    lax.fori_loop(0, blocks, finish, 0)
    results = Results(head, outs, stage, out_sems)
    all_docs(blocks, longest, me * 4, docs, keys_held, held, prob, dsc, results)


def attend(kernel, sources, previous, order, docs, rows, blocks, longest, heads, gathered):
    out_shape = [jax.ShapeDtypeStruct((rows, heads * HEAD_DIM), jnp.bfloat16)] * 3
    out_specs = [ANY] * 3
    held = (ARRAYS - 1, blocks * BLOCK, HEAD_DIM)
    first = 2 + len(sources)
    aliases = {first + i: i for i in range(len(previous))}
    scratch = [
        pltpu.VMEM((longest * BLOCK, longest * BLOCK), jnp.bfloat16),
        pltpu.VMEM((longest * BLOCK, longest * BLOCK), jnp.bfloat16),
        pltpu.VMEM((3, 4 * BLOCK, HEAD_DIM), jnp.bfloat16),
        pltpu.SemaphoreType.DMA((3,)),
        pltpu.VMEM((blocks * BLOCK, HEAD_DIM), jnp.bfloat16),
    ]
    if gathered:
        scratch += [pltpu.VMEM(held, jnp.bfloat16), pltpu.SemaphoreType.DMA((blocks * ARRAYS,))]
    else:
        out_shape.append(jax.ShapeDtypeStruct(held, jnp.bfloat16))
        out_specs.append(VMEM)
        aliases[2] = 3
    return pl.pallas_call(
        kernel,
        out_shape=out_shape,
        in_specs=[SMEM, SMEM] + [ANY if gathered else VMEM] * len(sources) + [ANY] * len(previous),
        out_specs=out_specs,
        scratch_shapes=scratch,
        input_output_aliases=aliases,
        compiler_params=pltpu.CompilerParams(vmem_limit_bytes=(60 if gathered else 32) << 20),
        cost_estimate=pl.CostEstimate(
            flops=10**6, bytes_accessed=10**4, transcendentals=10**3
        ),
        name="attend",
    )(order, docs, *sources, *previous)[:3]


def local(queries, keys, values, grad_out, block_docs, block_order):
    rows, width = queries.shape
    heads = width // HEAD_DIM
    blocks = block_order.shape[0]
    longest = blocks * 3 // 8
    arrays = (keys, values, queries, grad_out)
    grads = ()
    if lax.axis_size("ctx") != 4 or blocks != 16 or heads != 2:
        whole = [lax.all_gather(x, "ctx", axis=0, tiled=True) for x in arrays]
        for head in range(heads):
            grads = attend(
                functools.partial(attend_gathered, blocks, longest, head),
                whole, grads, block_order, block_docs, rows, blocks, longest, heads, True,
            )
        return tuple(grads)

    def swap(array, flip):
        return lax.ppermute(array, "ctx", [(i, i ^ flip) for i in range(4)])

    key_row = swap(keys, 2)
    core = [swap(x, 1) for x in arrays]
    shapes = [(slots, 3, BLOCK, HEAD_DIM) for slots in (2, 2, 3)] + [(3, blocks * BLOCK, HEAD_DIM)] * 2
    *packed, held0, held1 = pl.pallas_call(
        pack_slots,
        out_shape=[jax.ShapeDtypeStruct(shape, jnp.bfloat16) for shape in shapes],
        in_specs=[SMEM] * 2 + [VMEM] * 6,
        out_specs=[VMEM] * 5,
        compiler_params=pltpu.CompilerParams(vmem_limit_bytes=16 << 20),
        name="pack",
    )(block_order, block_docs, *arrays[1:], *core[1:])
    row = [swap(x, 2) for x in packed]
    all_keys = (keys, core[0], key_row, swap(key_row, 1))
    diag = [swap(x, 1) for x in row[:2]]
    far = (row[1], diag[1])
    grads = attend(
        functools.partial(attend_slots, blocks, longest, 0),
        (held0, *all_keys, *far, *row[:2], *diag), (), block_order, block_docs, rows, blocks, longest, heads, False,
    )
    last, grads = lax.optimization_barrier((row[2], grads))
    grads = attend(
        functools.partial(attend_slots, blocks, longest, 1),
        (held1, *all_keys, *far, last, swap(last, 1)), grads, block_order, block_docs, rows, blocks, longest, heads, False,
    )
    return tuple(grads)


def solution(mesh):
    rows = P(("grp", "ctx"), "head")
    return jax.shard_map(
        local,
        mesh=mesh,
        in_specs=(rows, rows, rows, rows, P("grp"), P("grp")),
        out_specs=(rows, rows, rows),
        check_vma=False,
    )
```

```python
import functools

import jax
import jax.numpy as jnp
import numpy as np
from jax import lax
from jax.experimental import pallas as pl
from jax.experimental.pallas import tpu as pltpu
from jax.sharding import PartitionSpec as P

HEAD_DIM = 128
BLOCK = 128
ARRAYS = 4
NEG_FILL = -1e30
SCALE = HEAD_DIM**-0.5
EXP2_SCALE = SCALE * float(np.log2(np.e))
NT = (((1,), (1,)), ((), ()))
TN = (((0,), (0,)), ((), ()))
NN = (((1,), (0,)), ((), ()))
ANY = pl.BlockSpec(memory_space=pl.ANY)
VMEM = pl.BlockSpec(memory_space=pltpu.VMEM)
SMEM = pl.BlockSpec(memory_space=pltpu.SMEM)


def dot(a, b, dims):
    return lax.dot_general(a, b, dims, preferred_element_type=jnp.float32)


def position_of(order, device, group):
    place = jnp.int32(0)
    block = jnp.int32(0)
    for j in range(4):
        candidate = order[device * 4 + j]
        hit = candidate // 4 == group
        place = jnp.where(hit, j, place)
        block = jnp.where(hit, candidate, block)
    return place, block


def slot_group(device, slot):
    return jnp.where(device // 2 == 0, (2, 3, 1)[slot], (1, 0, 2)[slot])


def far_block(device):
    return jnp.where(device // 2 == 0, 3, 12)


def rows_of(block):
    return pl.ds(pl.multiple_of(block * BLOCK, BLOCK), BLOCK)


def columns_of(head):
    return slice(head * HEAD_DIM, (head + 1) * HEAD_DIM)


def pack_slots(order, *refs):
    own, core, outs, held = refs[:3], refs[3:6], refs[6:9], refs[9:]
    me = lax.axis_index("ctx")
    for slot in range(3):
        place, _ = position_of(order, me, slot_group(me, slot))
        for array in range(3):
            outs[slot // 2][slot % 2, array] = own[array][rows_of(place), columns_of(0)]
            outs[2][slot, array] = own[array][rows_of(place), columns_of(1)]
    for sources, device in ((own, me), (core, me ^ 1)):
        for j in range(4):
            block = order[device * 4 + j]
            rows = slice(j * BLOCK, (j + 1) * BLOCK)
            for head in range(2):

                @pl.when((block == far_block(me)) & (me % 2 == head))
                def _(sources=sources, rows=rows, head=head):
                    for array in range(3):
                        outs[1][1, array] = sources[array][rows, columns_of(head)]
            for array in range(3):
                for head in range(2):
                    held[head][array, rows_of(block), :] = sources[array][rows, columns_of(head)]


def one_doc(length, exact, start, end, base, blocks, keys_held, held, prob, dsc, results):
    window = start if exact else jnp.minimum(start, blocks - length)
    rows = length * BLOCK
    whole = pl.ds(pl.multiple_of(window * BLOCK, BLOCK), rows)
    keys = keys_held[whole, :]
    values = held[0, whole, :]
    pair = min(3 if exact else 2, length)
    if not exact:
        key_block = window + lax.broadcasted_iota(jnp.int32, (rows, pair * BLOCK), 0) // BLOCK
        key_ok = (key_block >= start) & (key_block < end)

    def stats(first):
        at = window + first
        these = pl.ds(pl.multiple_of(at * BLOCK, BLOCK), pair * BLOCK)
        queries = held[1, these, :]
        douts = held[2, these, :]
        scores = dot(keys, queries, NT) * EXP2_SCALE
        dprob = dot(values, douts, NT)
        if not exact:
            scores = jnp.where(key_ok, scores, NEG_FILL)
        top = jnp.max(scores, axis=0, keepdims=True)
        weights = jnp.exp2(scores - top)
        inverse = 1.0 / jnp.sum(weights, axis=0, keepdims=True)
        probabilities = weights * inverse
        delta = jnp.sum(probabilities * dprob, axis=0, keepdims=True)
        dscore = probabilities * (dprob - delta)
        if not exact:
            query_block = at + lax.broadcasted_iota(jnp.int32, (rows, pair * BLOCK), 1) // BLOCK
            ok = key_ok & (query_block >= start) & (query_block < end)
            probabilities = jnp.where(ok, probabilities, 0.0)
            dscore = jnp.where(ok, dscore, 0.0)
        return probabilities.astype(jnp.bfloat16), dscore.astype(jnp.bfloat16)

    queries = held[1, whole, :]
    douts = held[2, whole, :]

    def store(first, count, prob_rows, dsc_rows, dsc_columns):
        def put(array, value):
            results.stage[array, results.rows(first - base, count), :] = value.astype(jnp.bfloat16)
            results.copy(array, first - base, count).start()

        put(2, dot(prob_rows, douts, NN))
        put(1, dot(dsc_rows, queries, NN) * SCALE)
        put(0, dot(dsc_columns, keys, TN) * SCALE)

    if exact and length <= 2:
        prob_low, dsc_low = stats(0)
        for i in range(length):
            mine = slice(i * BLOCK, (i + 1) * BLOCK)
            block = start + i
            pl.when((block >= base) & (block < base + 4))(
                functools.partial(store, block, 1, prob_low[mine], dsc_low[mine], dsc_low[:, mine])
            )
        return

    def fill(first):
        at = first * BLOCK
        columns = pl.ds(at if exact else pl.multiple_of(at, BLOCK), pair * BLOCK)
        prob[0:rows, columns], dsc[0:rows, columns] = stats(first)

    if exact:
        for step in range(-(-length // pair)):
            fill(min(step * pair, length - pair))
    else:

        @pl.loop(0, -(-length // pair))
        def _(step):
            fill(jnp.minimum(step * pair, length - pair))
    first = jnp.maximum(start, base)
    owned = jnp.minimum(end, base + 4) - first
    mine = pl.multiple_of((first - window) * BLOCK, BLOCK)
    for count in range(1, min(4, length) + 1):

        @pl.when(owned == count)
        def _(count=count):
            these = pl.ds(mine, count * BLOCK)
            store(first, count, prob[these, 0:rows], dsc[these, 0:rows], dsc[0:rows, these])


class Results:
    def __init__(self, head, outs, stage, sems):
        self.head, self.outs, self.stage, self.sems = head, outs, stage, sems

    def rows(self, at, count):
        return pl.ds(pl.multiple_of(at * BLOCK, BLOCK), count * BLOCK)

    def copy(self, array, at, count):
        rows = self.rows(at, count)
        return pltpu.make_async_copy(
            self.stage.at[array, rows, :],
            self.outs[array].at[rows, pl.ds(self.head * HEAD_DIM, HEAD_DIM)],
            self.sems.at[array],
        )


def all_docs(blocks, longest, base, docs, keys_held, held, prob, dsc, results):
    if longest <= 8:
        sizes = list(range(1, longest + 1))
    else:
        step = -(-longest // 6)
        sizes = [min(longest, step * (i + 1)) for i in range(-(-longest // step))]

    def visit(t, carry):
        block = base + t
        doc = docs[block]
        begins = jnp.logical_or(t == 0, docs[jnp.maximum(block - 1, 0)] != doc)

        @pl.when(begins)
        def _():
            start, end = jnp.int32(0), jnp.int32(0)
            for b in range(blocks):
                other = docs[b]
                start += (other < doc).astype(jnp.int32)
                end += (other <= doc).astype(jnp.int32)
            length = end - start
            below = 0
            for size in sizes:
                pl.when((length > below) & (length <= size))(
                    functools.partial(
                        one_doc, size, size - below == 1, start, end, base, blocks, keys_held, held, prob, dsc, results
                    )
                )
                below = size

        return carry

    lax.fori_loop(0, 4, visit, 0)
    for array in range(3):
        results.copy(array, 0, 4).wait()


def attend_slots(blocks, longest, head, order, docs, *refs):
    keys, (far_row, far_diag) = refs[1:5], refs[5:7]
    row, diag = (refs[7:9], refs[9:11]) if head == 0 else (refs[7:8], refs[8:9])
    outs, held, (prob, dsc, stage, sems, keys_held) = refs[-9:-6], refs[-6], refs[-5:]
    me = lax.axis_index("ctx")
    other = me ^ 2

    for flip, source in enumerate(keys):
        for j in range(4):
            to = rows_of(order[(me ^ flip) * 4 + j])
            keys_held[to, :] = source[j * BLOCK : (j + 1) * BLOCK, columns_of(head)]

    def bring(block, source, at):
        for array in range(3):
            held[array, rows_of(block), :] = source[at, array]

    for slot in range(3):
        for device, pieces in ((other, row), (other ^ 1, diag)):
            _, block = position_of(order, device, slot_group(device, slot))
            bring(block, pieces[slot // pieces[0].shape[0]], slot % pieces[0].shape[0])
    block = far_block(other)
    held_there = order[other // 2 * 8] == block
    for position in range(1, 8):
        held_there |= order[other // 2 * 8 + position] == block
    for source, core_of in ((far_row, head), (far_diag, 1 - head)):
        pl.when(held_there & (me % 2 == core_of))(
            functools.partial(bring, block, source, source.shape[0] - 1)
        )

    all_docs(blocks, longest, me * 4, docs, keys_held, held, prob, dsc, Results(head, outs, stage, sems))


def attend_gathered(blocks, longest, head, order, docs, keys, values, queries, grad_out, *rest):
    outs, (prob, dsc, stage, out_sems, keys_held, held, sems) = rest[-10:-7], rest[-7:]
    me = lax.axis_index("ctx")

    def copies(position):
        rows = pl.ds(pl.multiple_of(position * BLOCK, BLOCK), BLOCK)
        to = pl.ds(pl.multiple_of(order[position] * BLOCK, BLOCK), BLOCK)
        return [
            pltpu.make_async_copy(
                source.at[rows, pl.ds(head * HEAD_DIM, HEAD_DIM)],
                keys_held.at[to, :] if array == 0 else held.at[array - 1, to, :],
                sems.at[position * ARRAYS + array],
            )
            for array, source in enumerate((keys, values, queries, grad_out))
        ]

    def begin(position, carry):
        for copy in copies(position):
            copy.start()
        return carry

    def finish(position, carry):
        for copy in copies(position):
            copy.wait()
        return carry

    lax.fori_loop(0, blocks, begin, 0)
    lax.fori_loop(0, blocks, finish, 0)
    results = Results(head, outs, stage, out_sems)
    all_docs(blocks, longest, me * 4, docs, keys_held, held, prob, dsc, results)


def attend(kernel, sources, previous, order, docs, rows, blocks, longest, heads, gathered):
    out_shape = [jax.ShapeDtypeStruct((rows, heads * HEAD_DIM), jnp.bfloat16)] * 3
    out_specs = [ANY] * 3
    held = (ARRAYS - 1, blocks * BLOCK, HEAD_DIM)
    first = 2 + len(sources)
    aliases = {first + i: i for i in range(len(previous))}
    scratch = [
        pltpu.VMEM((longest * BLOCK, longest * BLOCK), jnp.bfloat16),
        pltpu.VMEM((longest * BLOCK, longest * BLOCK), jnp.bfloat16),
        pltpu.VMEM((3, 4 * BLOCK, HEAD_DIM), jnp.bfloat16),
        pltpu.SemaphoreType.DMA((3,)),
        pltpu.VMEM((blocks * BLOCK, HEAD_DIM), jnp.bfloat16),
    ]
    if gathered:
        scratch += [pltpu.VMEM(held, jnp.bfloat16), pltpu.SemaphoreType.DMA((blocks * ARRAYS,))]
    else:
        out_shape.append(jax.ShapeDtypeStruct(held, jnp.bfloat16))
        out_specs.append(VMEM)
        aliases[2] = 3
    return pl.pallas_call(
        kernel,
        out_shape=out_shape,
        in_specs=[SMEM, SMEM] + [ANY if gathered else VMEM] * len(sources) + [ANY] * len(previous),
        out_specs=out_specs,
        scratch_shapes=scratch,
        input_output_aliases=aliases,
        compiler_params=pltpu.CompilerParams(vmem_limit_bytes=(60 if gathered else 32) << 20),
        cost_estimate=pl.CostEstimate(
            flops=10**6, bytes_accessed=10**4, transcendentals=10**3
        ),
        name="attend",
    )(order, docs, *sources, *previous)[:3]


def local(queries, keys, values, grad_out, block_docs, block_order):
    rows, width = queries.shape
    heads = width // HEAD_DIM
    blocks = block_order.shape[0]
    longest = blocks * 3 // 8
    arrays = (keys, values, queries, grad_out)
    grads = ()
    if lax.axis_size("ctx") != 4 or blocks != 16 or heads != 2:
        whole = [lax.all_gather(x, "ctx", axis=0, tiled=True) for x in arrays]
        for head in range(heads):
            grads = attend(
                functools.partial(attend_gathered, blocks, longest, head),
                whole, grads, block_order, block_docs, rows, blocks, longest, heads, True,
            )
        return tuple(grads)

    def swap(array, flip):
        return lax.ppermute(array, "ctx", [(i, i ^ flip) for i in range(4)])

    key_row = swap(keys, 2)
    core = [swap(x, 1) for x in arrays]
    shapes = [(slots, 3, BLOCK, HEAD_DIM) for slots in (2, 2, 3)] + [(3, blocks * BLOCK, HEAD_DIM)] * 2
    *packed, held0, held1 = pl.pallas_call(
        pack_slots,
        out_shape=[jax.ShapeDtypeStruct(shape, jnp.bfloat16) for shape in shapes],
        in_specs=[SMEM] + [VMEM] * 6,
        out_specs=[VMEM] * 5,
        compiler_params=pltpu.CompilerParams(vmem_limit_bytes=16 << 20),
        name="pack",
    )(block_order, *arrays[1:], *core[1:])
    row = [swap(x, 2) for x in packed]
    all_keys = (keys, core[0], key_row, swap(key_row, 1))
    diag = [swap(x, 1) for x in row[:2]]
    far = (row[1], diag[1])
    grads = attend(
        functools.partial(attend_slots, blocks, longest, 0),
        (held0, *all_keys, *far, *row[:2], *diag), (), block_order, block_docs, rows, blocks, longest, heads, False,
    )
    last, grads = lax.optimization_barrier((row[2], grads))
    grads = attend(
        functools.partial(attend_slots, blocks, longest, 1),
        (held1, *all_keys, *far, last, swap(last, 1)), grads, block_order, block_docs, rows, blocks, longest, heads, False,
    )
    return tuple(grads)


def solution(mesh):
    rows = P(("grp", "ctx"), "head")
    return jax.shard_map(
        local,
        mesh=mesh,
        in_specs=(rows, rows, rows, rows, P("grp"), P("grp")),
        out_specs=(rows, rows, rows),
        check_vma=False,
    )
```

```python
import functools

import jax
import jax.numpy as jnp
import numpy as np
from jax import lax
from jax.experimental import pallas as pl
from jax.experimental.pallas import tpu as pltpu
from jax.sharding import PartitionSpec as P

HEAD_DIM = 128
BLOCK = 128
ARRAYS = 4
NEG_FILL = -1e30
SCALE = HEAD_DIM**-0.5
EXP2_SCALE = SCALE * float(np.log2(np.e))
NT = (((1,), (1,)), ((), ()))
TN = (((0,), (0,)), ((), ()))
NN = (((1,), (0,)), ((), ()))
ANY = pl.BlockSpec(memory_space=pl.ANY)
VMEM = pl.BlockSpec(memory_space=pltpu.VMEM)
SMEM = pl.BlockSpec(memory_space=pltpu.SMEM)


def dot(a, b, dims):
    return lax.dot_general(a, b, dims, preferred_element_type=jnp.float32)


def position_of(order, device, group):
    place = jnp.int32(0)
    block = jnp.int32(0)
    for j in range(4):
        candidate = order[device * 4 + j]
        hit = candidate // 4 == group
        place = jnp.where(hit, j, place)
        block = jnp.where(hit, candidate, block)
    return place, block


def slot_group(device, slot):
    return jnp.where(device // 2 == 0, (2, 3, 1)[slot], (1, 0, 2)[slot])


def far_block(device):
    return jnp.where(device // 2 == 0, 3, 12)


def rows_of(block):
    return pl.ds(pl.multiple_of(block * BLOCK, BLOCK), BLOCK)


def columns_of(head):
    return slice(head * HEAD_DIM, (head + 1) * HEAD_DIM)


def pack_slots(order, *refs):
    own, core, outs, held = refs[:3], refs[3:6], refs[6:9], refs[9:]
    me = lax.axis_index("ctx")
    for slot in range(3):
        place, _ = position_of(order, me, slot_group(me, slot))
        for array in range(3):
            outs[slot // 2][slot % 2, array] = own[array][rows_of(place), columns_of(0)]
            outs[2][slot, array] = own[array][rows_of(place), columns_of(1)]
    for sources, device in ((own, me), (core, me ^ 1)):
        for j in range(4):
            block = order[device * 4 + j]
            rows = slice(j * BLOCK, (j + 1) * BLOCK)
            for head in range(2):

                @pl.when((block == far_block(me)) & (me % 2 == head))
                def _(sources=sources, rows=rows, head=head):
                    for array in range(3):
                        outs[1][1, array] = sources[array][rows, columns_of(head)]
            for array in range(3):
                for head in range(2):
                    held[head][array, rows_of(block), :] = sources[array][rows, columns_of(head)]


def one_doc(length, exact, start, end, base, blocks, keys_held, held, prob, dsc, results):
    window = start if exact else jnp.minimum(start, blocks - length)
    rows = length * BLOCK
    whole = pl.ds(pl.multiple_of(window * BLOCK, BLOCK), rows)
    keys = keys_held[whole, :]
    values = held[0, whole, :]
    pair = min(2, length)
    if not exact:
        key_block = window + lax.broadcasted_iota(jnp.int32, (rows, pair * BLOCK), 0) // BLOCK
        key_ok = (key_block >= start) & (key_block < end)

    def stats(first, count):
        at = window + first
        these = pl.ds(pl.multiple_of(at * BLOCK, BLOCK), count * BLOCK)
        queries = held[1, these, :]
        douts = held[2, these, :]
        scores = dot(keys, queries, NT) * EXP2_SCALE
        dprob = dot(values, douts, NT)
        if not exact:
            scores = jnp.where(key_ok, scores, NEG_FILL)
        top = jnp.max(scores, axis=0, keepdims=True)
        weights = jnp.exp2(scores - top)
        inverse = 1.0 / jnp.sum(weights, axis=0, keepdims=True)
        probabilities = weights * inverse
        delta = jnp.sum(probabilities * dprob, axis=0, keepdims=True)
        dscore = probabilities * (dprob - delta)
        if not exact:
            query_block = at + lax.broadcasted_iota(jnp.int32, (rows, count * BLOCK), 1) // BLOCK
            ok = key_ok & (query_block >= start) & (query_block < end)
            probabilities = jnp.where(ok, probabilities, 0.0)
            dscore = jnp.where(ok, dscore, 0.0)
        return probabilities.astype(jnp.bfloat16), dscore.astype(jnp.bfloat16)

    queries = held[1, whole, :]
    douts = held[2, whole, :]

    def store(first, count, prob_rows, dsc_rows, dsc_columns):
        at = first - base
        results.put(2, at, count, dot(prob_rows, douts, NN))
        results.put(1, at, count, dot(dsc_rows, queries, NN) * SCALE)
        results.put(0, at, count, dot(dsc_columns, keys, TN) * SCALE)

    if exact and length <= 2:
        prob_low, dsc_low = stats(0, length)
        for i in range(length):
            mine = slice(i * BLOCK, (i + 1) * BLOCK)
            block = start + i
            pl.when((block >= base) & (block < base + 4))(
                functools.partial(store, block, 1, prob_low[mine], dsc_low[mine], dsc_low[:, mine])
            )
        return

    def fill(first, count):
        at = first * BLOCK
        columns = pl.ds(at if exact else pl.multiple_of(at, BLOCK), count * BLOCK)
        prob[0:rows, columns], dsc[0:rows, columns] = stats(first, count)

    if exact:
        half = -(-length // 2)
        fill(0, half)
        fill(half, length - half)
    else:

        @pl.loop(0, -(-length // pair))
        def _(step):
            fill(jnp.minimum(step * pair, length - pair), pair)

    first = jnp.maximum(start, base)
    owned = jnp.minimum(end, base + 4) - first
    mine = pl.multiple_of((first - window) * BLOCK, BLOCK)
    for count in range(1, min(4, length) + 1):

        @pl.when(owned == count)
        def _(count=count):
            these = pl.ds(mine, count * BLOCK)
            store(first, count, prob[these, 0:rows], dsc[these, 0:rows], dsc[0:rows, these])


class Results:
    def __init__(self, head, outs, stage, sems):
        self.head, self.outs, self.stage, self.sems = head, outs, stage, sems

    def rows(self, at, count):
        return pl.ds(pl.multiple_of(at * BLOCK, BLOCK), count * BLOCK)

    def put(self, array, at, count, value):
        self.stage[array, self.rows(at, count), :] = value.astype(jnp.bfloat16)
        if self.outs:
            self.copy(array, at, count).start()

    def start(self):
        for array in range(3):
            self.copy(array, 0, 4).start()

    def wait(self):
        if self.outs:
            for array in range(3):
                self.copy(array, 0, 4).wait()

    def copy(self, array, at, count):
        rows = self.rows(at, count)
        return pltpu.make_async_copy(
            self.stage.at[array, rows, :],
            self.outs[array].at[rows, pl.ds(self.head * HEAD_DIM, HEAD_DIM)],
            self.sems.at[array],
        )


def all_docs(blocks, longest, base, docs, keys_held, held, prob, dsc, results):
    if longest <= 8:
        sizes = list(range(1, longest + 1))
    else:
        step = -(-longest // 6)
        sizes = [min(longest, step * (i + 1)) for i in range(-(-longest // step))]

    def visit(t, carry):
        block = base + t
        doc = docs[block]
        begins = jnp.logical_or(t == 0, docs[jnp.maximum(block - 1, 0)] != doc)

        @pl.when(begins)
        def _():
            start, end = jnp.int32(0), jnp.int32(0)
            for b in range(blocks):
                other = docs[b]
                start += (other < doc).astype(jnp.int32)
                end += (other <= doc).astype(jnp.int32)
            length = end - start
            below = 0
            for size in sizes:
                pl.when((length > below) & (length <= size))(
                    functools.partial(
                        one_doc, size, size - below == 1, start, end, base, blocks, keys_held, held, prob, dsc, results
                    )
                )
                below = size

        return carry

    lax.fori_loop(0, 4, visit, 0)
    results.wait()


def attend_slots(blocks, longest, head, order, docs, *refs):
    keys, (far_row, far_diag) = refs[1:5], refs[5:7]
    if head == 0:
        row, diag = refs[7:9], refs[9:11]
        stage, held, prob, dsc, keys_held = refs[-5:]
        results = Results(0, (), stage, None)
    else:
        row, diag, before = refs[7:8], refs[8:9], refs[9]
        outs, (held, prob, dsc, keys_held, stage, sems) = refs[-9:-6], refs[-6:]
        earlier = Results(0, outs, before, sems.at[pl.ds(3, 3)])
        earlier.start()
        results = Results(1, outs, stage, sems)
    me = lax.axis_index("ctx")
    other = me ^ 2

    for flip, source in enumerate(keys):
        for j in range(4):
            to = rows_of(order[(me ^ flip) * 4 + j])
            keys_held[to, :] = source[j * BLOCK : (j + 1) * BLOCK, columns_of(head)]

    def bring(block, source, at):
        for array in range(3):
            held[array, rows_of(block), :] = source[at, array]

    for slot in range(3):
        for device, pieces in ((other, row), (other ^ 1, diag)):
            _, block = position_of(order, device, slot_group(device, slot))
            bring(block, pieces[slot // pieces[0].shape[0]], slot % pieces[0].shape[0])
    block = far_block(other)
    held_there = order[other // 2 * 8] == block
    for position in range(1, 8):
        held_there |= order[other // 2 * 8 + position] == block
    for source, core_of in ((far_row, head), (far_diag, 1 - head)):
        pl.when(held_there & (me % 2 == core_of))(
            functools.partial(bring, block, source, source.shape[0] - 1)
        )

    all_docs(blocks, longest, me * 4, docs, keys_held, held, prob, dsc, results)
    if head:
        earlier.wait()


def attend_gathered(blocks, longest, head, order, docs, keys, values, queries, grad_out, *rest):
    outs, (prob, dsc, keys_held, stage, out_sems, held, sems) = rest[-10:-7], rest[-7:]
    me = lax.axis_index("ctx")

    def copies(position):
        rows = pl.ds(pl.multiple_of(position * BLOCK, BLOCK), BLOCK)
        to = pl.ds(pl.multiple_of(order[position] * BLOCK, BLOCK), BLOCK)
        return [
            pltpu.make_async_copy(
                source.at[rows, pl.ds(head * HEAD_DIM, HEAD_DIM)],
                keys_held.at[to, :] if array == 0 else held.at[array - 1, to, :],
                sems.at[position * ARRAYS + array],
            )
            for array, source in enumerate((keys, values, queries, grad_out))
        ]

    def begin(position, carry):
        for copy in copies(position):
            copy.start()
        return carry

    def finish(position, carry):
        for copy in copies(position):
            copy.wait()
        return carry

    lax.fori_loop(0, blocks, begin, 0)
    lax.fori_loop(0, blocks, finish, 0)
    results = Results(head, outs, stage, out_sems)
    all_docs(blocks, longest, me * 4, docs, keys_held, held, prob, dsc, results)


def attend(kernel, sources, previous, order, docs, rows, blocks, longest, heads, gathered, last=True):
    staged = (3, 4 * BLOCK, HEAD_DIM)
    held = (ARRAYS - 1, blocks * BLOCK, HEAD_DIM)
    shapes = [(rows, heads * HEAD_DIM)] * 3 if last else [staged]
    out_specs = [ANY] * 3 if last else [VMEM]
    first = 2 + len(sources)
    aliases = {first + i: i for i in range(len(previous))}
    scratch = [
        pltpu.VMEM((longest * BLOCK, longest * BLOCK), jnp.bfloat16),
        pltpu.VMEM((longest * BLOCK, longest * BLOCK), jnp.bfloat16),
        pltpu.VMEM((blocks * BLOCK, HEAD_DIM), jnp.bfloat16),
    ]
    if last:
        scratch += [pltpu.VMEM(staged, jnp.bfloat16), pltpu.SemaphoreType.DMA((6,))]
    if gathered:
        scratch += [pltpu.VMEM(held, jnp.bfloat16), pltpu.SemaphoreType.DMA((blocks * ARRAYS,))]
    else:
        aliases[2] = len(shapes)
        shapes.append(held)
        out_specs.append(VMEM)
    return pl.pallas_call(
        kernel,
        out_shape=[jax.ShapeDtypeStruct(shape, jnp.bfloat16) for shape in shapes],
        in_specs=[SMEM, SMEM] + [ANY if gathered else VMEM] * len(sources) + [ANY] * len(previous),
        out_specs=out_specs,
        scratch_shapes=scratch,
        input_output_aliases=aliases,
        compiler_params=pltpu.CompilerParams(vmem_limit_bytes=(60 if gathered else 32) << 20),
        cost_estimate=pl.CostEstimate(
            flops=10**6, bytes_accessed=10**4, transcendentals=10**3
        ),
        name="attend",
    )(order, docs, *sources, *previous)


def local(queries, keys, values, grad_out, block_docs, block_order):
    rows, width = queries.shape
    heads = width // HEAD_DIM
    blocks = block_order.shape[0]
    longest = blocks * 3 // 8
    arrays = (keys, values, queries, grad_out)
    grads = ()
    if lax.axis_size("ctx") != 4 or blocks != 16 or heads != 2:
        whole = [lax.all_gather(x, "ctx", axis=0, tiled=True) for x in arrays]
        for head in range(heads):
            grads = attend(
                functools.partial(attend_gathered, blocks, longest, head),
                whole, grads, block_order, block_docs, rows, blocks, longest, heads, True,
            )
        return tuple(grads)

    def swap(array, flip):
        return lax.ppermute(array, "ctx", [(i, i ^ flip) for i in range(4)])

    key_row = swap(keys, 2)
    core = [swap(x, 1) for x in arrays]
    shapes = [(slots, 3, BLOCK, HEAD_DIM) for slots in (2, 2, 3)] + [(3, blocks * BLOCK, HEAD_DIM)] * 2
    *packed, held0, held1 = pl.pallas_call(
        pack_slots,
        out_shape=[jax.ShapeDtypeStruct(shape, jnp.bfloat16) for shape in shapes],
        in_specs=[SMEM] + [VMEM] * 6,
        out_specs=[VMEM] * 5,
        compiler_params=pltpu.CompilerParams(vmem_limit_bytes=16 << 20),
        name="pack",
    )(block_order, *arrays[1:], *core[1:])
    row = [swap(x, 2) for x in packed]
    all_keys = (keys, core[0], key_row, swap(key_row, 1))
    diag = [swap(x, 1) for x in row[:2]]
    far = (row[1], diag[1])
    sizes = (block_order, block_docs, rows, blocks, longest, heads, False)
    before = attend(
        functools.partial(attend_slots, blocks, longest, 0),
        (held0, *all_keys, *far, *row[:2], *diag), (), *sizes, last=False,
    )[0]
    last, before = lax.optimization_barrier((row[2], before))
    grads = attend(
        functools.partial(attend_slots, blocks, longest, 1),
        (held1, *all_keys, *far, last, swap(last, 1), before), (), *sizes,
    )
    return tuple(grads[:3])


def solution(mesh):
    rows = P(("grp", "ctx"), "head")
    return jax.shard_map(
        local,
        mesh=mesh,
        in_specs=(rows, rows, rows, rows, P("grp"), P("grp")),
        out_specs=(rows, rows, rows),
        check_vma=False,
    )
```

```python
import functools

import jax
import jax.numpy as jnp
import numpy as np
from jax import lax
from jax.experimental import pallas as pl
from jax.experimental.pallas import tpu as pltpu
from jax.sharding import PartitionSpec as P

HEAD_DIM = 128
BLOCK = 128
ARRAYS = 4
NEG_FILL = -1e30
SCALE = HEAD_DIM**-0.5
EXP2_SCALE = SCALE * float(np.log2(np.e))
NT = (((1,), (1,)), ((), ()))
TN = (((0,), (0,)), ((), ()))
NN = (((1,), (0,)), ((), ()))
ANY = pl.BlockSpec(memory_space=pl.ANY)
VMEM = pl.BlockSpec(memory_space=pltpu.VMEM)
SMEM = pl.BlockSpec(memory_space=pltpu.SMEM)


def dot(a, b, dims):
    return lax.dot_general(a, b, dims, preferred_element_type=jnp.float32)


def position_of(order, device, group):
    place = jnp.int32(0)
    block = jnp.int32(0)
    for j in range(4):
        candidate = order[device * 4 + j]
        hit = candidate // 4 == group
        place = jnp.where(hit, j, place)
        block = jnp.where(hit, candidate, block)
    return place, block


def slot_group(device, slot):
    return jnp.where(device // 2 == 0, (2, 3, 1)[slot], (1, 0, 2)[slot])


def far_block(device):
    return jnp.where(device // 2 == 0, 3, 12)


def rows_of(block):
    return pl.ds(pl.multiple_of(block * BLOCK, BLOCK), BLOCK)


def columns_of(head):
    return slice(head * HEAD_DIM, (head + 1) * HEAD_DIM)


def pack_slots(order, *refs):
    own, core, outs, held = refs[:3], refs[3:6], refs[6:9], refs[9:]
    me = lax.axis_index("ctx")
    for slot in range(3):
        place, _ = position_of(order, me, slot_group(me, slot))
        for array in range(3):
            outs[slot // 2][slot % 2, array] = own[array][rows_of(place), columns_of(0)]
            outs[2][slot, array] = own[array][rows_of(place), columns_of(1)]
    for sources, device in ((own, me), (core, me ^ 1)):
        for j in range(4):
            block = order[device * 4 + j]
            rows = slice(j * BLOCK, (j + 1) * BLOCK)
            for head in range(2):

                @pl.when((block == far_block(me)) & (me % 2 == head))
                def _(sources=sources, rows=rows, head=head):
                    for array in range(3):
                        outs[1][1, array] = sources[array][rows, columns_of(head)]
            for array in range(3):
                for head in range(2):
                    held[head][array, rows_of(block), :] = sources[array][rows, columns_of(head)]


def one_doc(length, exact, start, end, base, blocks, keys_held, held, prob, dsc, results):
    window = start if exact else jnp.minimum(start, blocks - length)
    rows = length * BLOCK
    whole = pl.ds(pl.multiple_of(window * BLOCK, BLOCK), rows)
    keys = keys_held[whole, :]
    values = held[0, whole, :]
    pair = min(2, length)
    if not exact:
        key_block = window + lax.broadcasted_iota(jnp.int32, (rows, pair * BLOCK), 0) // BLOCK
        key_ok = (key_block >= start) & (key_block < end)

    def stats(first, count):
        at = window + first
        these = pl.ds(pl.multiple_of(at * BLOCK, BLOCK), count * BLOCK)
        queries = held[1, these, :]
        douts = held[2, these, :]
        scores = dot(keys, queries, NT) * EXP2_SCALE
        dprob = dot(values, douts, NT)
        if not exact:
            scores = jnp.where(key_ok, scores, NEG_FILL)
        top = jnp.max(scores, axis=0, keepdims=True)
        weights = jnp.exp2(scores - top)
        inverse = 1.0 / jnp.sum(weights, axis=0, keepdims=True)
        probabilities = weights * inverse
        delta = jnp.sum(probabilities * dprob, axis=0, keepdims=True)
        dscore = probabilities * (dprob - delta)
        if not exact:
            query_block = at + lax.broadcasted_iota(jnp.int32, (rows, count * BLOCK), 1) // BLOCK
            ok = key_ok & (query_block >= start) & (query_block < end)
            probabilities = jnp.where(ok, probabilities, 0.0)
            dscore = jnp.where(ok, dscore, 0.0)
        return probabilities.astype(jnp.bfloat16), dscore.astype(jnp.bfloat16)

    queries = held[1, whole, :]
    douts = held[2, whole, :]

    def store(first, count, prob_rows, dsc_rows, dsc_columns):
        at = first - base
        results.put(2, at, count, dot(prob_rows, douts, NN))
        results.put(1, at, count, dot(dsc_rows, queries, NN) * SCALE)
        half = -(-count // 2)
        for lo, hi in ((0, half), (half, count)):
            if hi > lo:
                part = dsc_columns[:, lo * BLOCK : hi * BLOCK]
                results.put(0, at + lo, hi - lo, dot(part, keys, TN) * SCALE)

    if exact and length <= 2:
        prob_low, dsc_low = stats(0, length)
        for i in range(length):
            mine = slice(i * BLOCK, (i + 1) * BLOCK)
            block = start + i
            pl.when((block >= base) & (block < base + 4))(
                functools.partial(store, block, 1, prob_low[mine], dsc_low[mine], dsc_low[:, mine])
            )
        return

    def fill(first, count):
        at = first * BLOCK
        columns = pl.ds(at if exact else pl.multiple_of(at, BLOCK), count * BLOCK)
        prob[0:rows, columns], dsc[0:rows, columns] = stats(first, count)

    if exact:
        half = -(-length // 2)
        fill(0, half)
        fill(half, length - half)
    else:

        @pl.loop(0, -(-length // pair))
        def _(step):
            fill(jnp.minimum(step * pair, length - pair), pair)

    first = jnp.maximum(start, base)
    owned = jnp.minimum(end, base + 4) - first
    mine = pl.multiple_of((first - window) * BLOCK, BLOCK)
    for count in range(1, min(4, length) + 1):

        @pl.when(owned == count)
        def _(count=count):
            these = pl.ds(mine, count * BLOCK)
            store(first, count, prob[these, 0:rows], dsc[these, 0:rows], dsc[0:rows, these])


class Results:
    def __init__(self, head, outs, stage, sems):
        self.head, self.outs, self.stage, self.sems = head, outs, stage, sems

    def rows(self, at, count):
        return pl.ds(pl.multiple_of(at * BLOCK, BLOCK), count * BLOCK)

    def put(self, array, at, count, value):
        self.stage[array, self.rows(at, count), :] = value.astype(jnp.bfloat16)
        if self.outs:
            self.copy(array, at, count).start()

    def start(self):
        for array in range(3):
            self.copy(array, 0, 4).start()

    def wait(self):
        if self.outs:
            for array in range(3):
                self.copy(array, 0, 4).wait()

    def copy(self, array, at, count):
        rows = self.rows(at, count)
        return pltpu.make_async_copy(
            self.stage.at[array, rows, :],
            self.outs[array].at[rows, pl.ds(self.head * HEAD_DIM, HEAD_DIM)],
            self.sems.at[array],
        )


def all_docs(blocks, longest, base, docs, keys_held, held, prob, dsc, results):
    if longest <= 8:
        sizes = list(range(1, longest + 1))
    else:
        step = -(-longest // 6)
        sizes = [min(longest, step * (i + 1)) for i in range(-(-longest // step))]

    def visit(t, carry):
        block = base + t
        doc = docs[block]
        begins = jnp.logical_or(t == 0, docs[jnp.maximum(block - 1, 0)] != doc)

        @pl.when(begins)
        def _():
            start, end = jnp.int32(0), jnp.int32(0)
            for b in range(blocks):
                other = docs[b]
                start += (other < doc).astype(jnp.int32)
                end += (other <= doc).astype(jnp.int32)
            length = end - start
            below = 0
            for size in sizes:
                pl.when((length > below) & (length <= size))(
                    functools.partial(
                        one_doc, size, size - below == 1, start, end, base, blocks, keys_held, held, prob, dsc, results
                    )
                )
                below = size

        return carry

    lax.fori_loop(0, 4, visit, 0)
    results.wait()


def attend_slots(blocks, longest, head, order, docs, *refs):
    keys, (far_row, far_diag) = refs[1:5], refs[5:7]
    if head == 0:
        row, diag = refs[7:9], refs[9:11]
        stage, held, prob, dsc, keys_held = refs[-5:]
        results = Results(0, (), stage, None)
    else:
        row, diag, before = refs[7:8], refs[8:9], refs[9]
        outs, (held, prob, dsc, keys_held, stage, sems) = refs[-9:-6], refs[-6:]
        earlier = Results(0, outs, before, sems.at[pl.ds(3, 3)])
        earlier.start()
        results = Results(1, outs, stage, sems)
    me = lax.axis_index("ctx")
    other = me ^ 2

    for flip, source in enumerate(keys):
        for j in range(4):
            to = rows_of(order[(me ^ flip) * 4 + j])
            keys_held[to, :] = source[j * BLOCK : (j + 1) * BLOCK, columns_of(head)]

    def bring(block, source, at):
        for array in range(3):
            held[array, rows_of(block), :] = source[at, array]

    for slot in range(3):
        for device, pieces in ((other, row), (other ^ 1, diag)):
            _, block = position_of(order, device, slot_group(device, slot))
            bring(block, pieces[slot // pieces[0].shape[0]], slot % pieces[0].shape[0])
    block = far_block(other)
    held_there = order[other // 2 * 8] == block
    for position in range(1, 8):
        held_there |= order[other // 2 * 8 + position] == block
    for source, core_of in ((far_row, head), (far_diag, 1 - head)):
        pl.when(held_there & (me % 2 == core_of))(
            functools.partial(bring, block, source, source.shape[0] - 1)
        )

    all_docs(blocks, longest, me * 4, docs, keys_held, held, prob, dsc, results)
    if head:
        earlier.wait()


def attend_gathered(blocks, longest, head, order, docs, keys, values, queries, grad_out, *rest):
    outs, (prob, dsc, keys_held, stage, out_sems, held, sems) = rest[-10:-7], rest[-7:]
    me = lax.axis_index("ctx")

    def copies(position):
        rows = pl.ds(pl.multiple_of(position * BLOCK, BLOCK), BLOCK)
        to = pl.ds(pl.multiple_of(order[position] * BLOCK, BLOCK), BLOCK)
        return [
            pltpu.make_async_copy(
                source.at[rows, pl.ds(head * HEAD_DIM, HEAD_DIM)],
                keys_held.at[to, :] if array == 0 else held.at[array - 1, to, :],
                sems.at[position * ARRAYS + array],
            )
            for array, source in enumerate((keys, values, queries, grad_out))
        ]

    def begin(position, carry):
        for copy in copies(position):
            copy.start()
        return carry

    def finish(position, carry):
        for copy in copies(position):
            copy.wait()
        return carry

    lax.fori_loop(0, blocks, begin, 0)
    lax.fori_loop(0, blocks, finish, 0)
    results = Results(head, outs, stage, out_sems)
    all_docs(blocks, longest, me * 4, docs, keys_held, held, prob, dsc, results)


def attend(kernel, sources, previous, order, docs, rows, blocks, longest, heads, gathered, last=True):
    staged = (3, 4 * BLOCK, HEAD_DIM)
    held = (ARRAYS - 1, blocks * BLOCK, HEAD_DIM)
    shapes = [(rows, heads * HEAD_DIM)] * 3 if last else [staged]
    out_specs = [ANY] * 3 if last else [VMEM]
    first = 2 + len(sources)
    aliases = {first + i: i for i in range(len(previous))}
    scratch = [
        pltpu.VMEM((longest * BLOCK, longest * BLOCK), jnp.bfloat16),
        pltpu.VMEM((longest * BLOCK, longest * BLOCK), jnp.bfloat16),
        pltpu.VMEM((blocks * BLOCK, HEAD_DIM), jnp.bfloat16),
    ]
    if last:
        scratch += [pltpu.VMEM(staged, jnp.bfloat16), pltpu.SemaphoreType.DMA((6,))]
    if gathered:
        scratch += [pltpu.VMEM(held, jnp.bfloat16), pltpu.SemaphoreType.DMA((blocks * ARRAYS,))]
    else:
        aliases[2] = len(shapes)
        shapes.append(held)
        out_specs.append(VMEM)
    return pl.pallas_call(
        kernel,
        out_shape=[jax.ShapeDtypeStruct(shape, jnp.bfloat16) for shape in shapes],
        in_specs=[SMEM, SMEM] + [ANY if gathered else VMEM] * len(sources) + [ANY] * len(previous),
        out_specs=out_specs,
        scratch_shapes=scratch,
        input_output_aliases=aliases,
        compiler_params=pltpu.CompilerParams(vmem_limit_bytes=(60 if gathered else 32) << 20),
        cost_estimate=pl.CostEstimate(
            flops=10**6, bytes_accessed=10**4, transcendentals=10**3
        ),
        name="attend",
    )(order, docs, *sources, *previous)


def local(queries, keys, values, grad_out, block_docs, block_order):
    rows, width = queries.shape
    heads = width // HEAD_DIM
    blocks = block_order.shape[0]
    longest = blocks * 3 // 8
    arrays = (keys, values, queries, grad_out)
    grads = ()
    if lax.axis_size("ctx") != 4 or blocks != 16 or heads != 2:
        whole = [lax.all_gather(x, "ctx", axis=0, tiled=True) for x in arrays]
        for head in range(heads):
            grads = attend(
                functools.partial(attend_gathered, blocks, longest, head),
                whole, grads, block_order, block_docs, rows, blocks, longest, heads, True,
            )
        return tuple(grads)

    def swap(array, flip):
        return lax.ppermute(array, "ctx", [(i, i ^ flip) for i in range(4)])

    key_row = swap(keys, 2)
    core = [swap(x, 1) for x in arrays]
    shapes = [(slots, 3, BLOCK, HEAD_DIM) for slots in (2, 2, 3)] + [(3, blocks * BLOCK, HEAD_DIM)] * 2
    *packed, held0, held1 = pl.pallas_call(
        pack_slots,
        out_shape=[jax.ShapeDtypeStruct(shape, jnp.bfloat16) for shape in shapes],
        in_specs=[SMEM] + [VMEM] * 6,
        out_specs=[VMEM] * 5,
        compiler_params=pltpu.CompilerParams(vmem_limit_bytes=16 << 20),
        name="pack",
    )(block_order, *arrays[1:], *core[1:])
    row = [swap(x, 2) for x in packed]
    all_keys = (keys, core[0], key_row, swap(key_row, 1))
    diag = [swap(x, 1) for x in row[:2]]
    far = (row[1], diag[1])
    sizes = (block_order, block_docs, rows, blocks, longest, heads, False)
    before = attend(
        functools.partial(attend_slots, blocks, longest, 0),
        (held0, *all_keys, *far, *row[:2], *diag), (), *sizes, last=False,
    )[0]
    last, before = lax.optimization_barrier((row[2], before))
    grads = attend(
        functools.partial(attend_slots, blocks, longest, 1),
        (held1, *all_keys, *far, last, swap(last, 1), before), (), *sizes,
    )
    return tuple(grads[:3])


def solution(mesh):
    rows = P(("grp", "ctx"), "head")
    return jax.shard_map(
        local,
        mesh=mesh,
        in_specs=(rows, rows, rows, rows, P("grp"), P("grp")),
        out_specs=(rows, rows, rows),
        check_vma=False,
    )
```
